128 devices in a mesh: seqo: 4 (over z), seqi: 16 (over y, x_hi, core), chan: 2 (over x_lo).
Axes of the slice: x: 4 (x_hi: 2, x_lo: 2; x = x_hi * 2 + x_lo), y: 4, z: 4, core: 2. Of those that a mesh axis runs over, the one named last changes fastest.
Arguments:
- signal: float32 [48, 524288], P('chan', ('seqo', 'seqi')), may hold values from -6 to 6
- cotangent: float32 [48, 524288], P('chan', ('seqo', 'seqi')), may hold values from -0.0078125 to 0.0078125
- long_filter: float32 [48, 524288], P('chan', ('seqo', 'seqi')), may hold values from -6 to 6
Outputs:
- grad_signal: float32 [48, 524288], P('chan', ('seqo', 'seqi'))
- grad_filter: float32 [48, 524288], P('chan', ('seqo', 'seqi'))
The draws below stay inside these ranges and needn't reach their ends.
All inputs are finite; a program needn't handle non-finite values.
Results may differ from the reference program's by a relative error of at most 0.000098.
Values sent between devices are 32-bit elements; how exact they have to be, the bound alone decides.
No kernel may reach another device: no remote copies, remote signals or barrier semaphores. Data moves between devices by JAX's collectives and lax.ppermute only.
A program may use at most 128 MiB of HBM per device.

```python
import jax
import jax.numpy as jnp
from jax import lax

CHANNELS = 48
SEQ = 524288


def level_of(rng, shape, pieces, smallest, largest):
    factor_of, own = 1.0, jax.random.fold_in(rng, 6)
    for position, parts in pieces:
        heights = jnp.exp(jax.random.uniform(jax.random.fold_in(own, position), (parts,), jnp.float32, smallest / len(pieces), largest / len(pieces)))
        factor_of = factor_of * jnp.repeat(heights, shape[position] // parts).reshape([-1 if axis == position else 1 for axis in range(len(shape))])
    return factor_of


def noise(rng, extent, deviation, reach, split=(), held_as=jnp.bfloat16):
    values = deviation * jax.random.normal(rng, extent, jnp.float32)
    if split:
        values = values * level_of(rng, extent, split, -0.22, 0.18)
    return jnp.clip(values, -reach, reach).astype(held_as)


def setup_inputs(seed: int = 0) -> dict:
    splits = jax.random.split(jax.random.key(seed), 4)
    return {
        "signal": noise(splits[0], (CHANNELS, SEQ), 1.0, 6.0, ((0, 2), (1, 64)), jnp.float32),
        "cotangent": noise(splits[1], (CHANNELS, SEQ), SEQ ** -0.5, 0.0078125, ((0, 2), (1, 64)), jnp.float32),
        "long_filter": noise(splits[2], (CHANNELS, SEQ), 1.0, 6.0, ((0, 2), (1, 64)), jnp.float32),
    }


def one_channel(rows):
    signal, cotangent, long_filter = rows
    padded_size = 2 * SEQ
    spec_signal = jnp.fft.rfft(signal, n=padded_size)
    spec_slope = jnp.fft.rfft(cotangent, n=padded_size)
    spec_filter = jnp.fft.rfft(long_filter, n=padded_size)
    source_spectrum = spec_slope * jnp.conj(spec_filter)
    kernel_spectrum = spec_slope * jnp.conj(spec_signal)
    grad_signal = jnp.fft.irfft(source_spectrum, n=padded_size)[:SEQ]
    grad_filter = jnp.fft.irfft(kernel_spectrum, n=padded_size)[:SEQ]
    return grad_signal.astype(jnp.float32), grad_filter.astype(jnp.float32)


def reference(signal, cotangent, long_filter):
    grad_signal, grad_filter = lax.map(one_channel, (signal, cotangent, long_filter))
    return grad_signal, grad_filter
```

```python
import functools
import math

import jax
import jax.numpy as jnp
import ml_dtypes
import numpy as np
from jax import lax
from jax.experimental import pallas as pl
from jax.experimental.pallas import tpu as pltpu
from jax.sharding import PartitionSpec as P

LANES = 128
OUTER = 64
GROUP = 8
ROOT_HALF = math.sqrt(0.5)


def unit(turns):
    return (math.cos(2.0 * math.pi * turns), math.sin(2.0 * math.pi * turns))


def plus(a, b):
    return (a[0] + b[0], a[1] + b[1])


def minus(a, b):
    return (a[0] - b[0], a[1] - b[1])


def turn(a, turns):
    turns = turns % 1.0
    if turns == 0.0:
        return a
    c, s = unit(turns)
    return (a[0] * c - a[1] * s, a[1] * c + a[0] * s)


def quarter(a, sign):
    if sign > 0:
        return (-a[1], a[0])
    return (a[1], -a[0])


def dft4(v, sign):
    t0, t1 = plus(v[0], v[2]), minus(v[0], v[2])
    t2, t3 = plus(v[1], v[3]), quarter(minus(v[1], v[3]), sign)
    return [plus(t0, t2), plus(t1, t3), minus(t0, t2), minus(t1, t3)]


def dft8(v, sign):
    up = [plus(v[n], v[n + 4]) for n in range(4)]
    down = [minus(v[n], v[n + 4]) for n in range(4)]
    r, i = down[1]
    down[1] = ((r - sign * i) * ROOT_HALF, (i + sign * r) * ROOT_HALF)
    down[2] = quarter(down[2], sign)
    r, i = down[3]
    down[3] = ((-r - sign * i) * ROOT_HALF, (sign * r - i) * ROOT_HALF)
    even, odd = dft4(up, sign), dft4(down, sign)
    return [even[k // 2] if k % 2 == 0 else odd[k // 2] for k in range(8)]


def load_pair(ref, *at):
    return (ref[(*at, slice(None), slice(0, LANES))], ref[(*at, slice(None), slice(LANES, 2 * LANES))])


def store_pair(ref, pair, *at):
    ref[(*at, slice(None), slice(0, LANES))] = pair[0]
    ref[(*at, slice(None), slice(LANES, 2 * LANES))] = pair[1]


def three_pass(rows, table):
    high = rows.astype(jnp.bfloat16)
    low = (rows - high.astype(jnp.float32)).astype(jnp.bfloat16)
    return jnp.dot(
        jnp.concatenate([high, low, high], axis=1), table, preferred_element_type=jnp.float32
    )


def forward_kernel(signal, cotangent, long_filter, phases, table, out, first, second):
    for number, source in enumerate((long_filter, signal, cotangent)):
        for b in range(8):
            column = []
            for a in range(8):
                x = source[:, (8 * a + b) * LANES : (8 * a + b + 1) * LANES]
                c, s = unit(-a / 32.0)
                column.append((x * c, x * s))
            for q, value in enumerate(dft8(column, -1)):
                store_pair(first, turn(value, -b * (q + 0.25) / 64.0), 8 * b + q)
        for q in range(8):
            column = [load_pair(first, 8 * b + q) for b in range(8)]
            for p, (r, i) in enumerate(dft8(column, -1)):
                at = q + 8 * p
                c = phases[at : at + 1, :LANES]
                s = phases[at : at + 1, LANES:]
                rows = slice(GROUP * number, GROUP * (number + 1))
                second[at, rows, :LANES] = r * c + i * s
                second[at, rows, LANES:] = i * c - r * s
    step = 8
    for at in range(0, OUTER, step):
        rows = second[at : at + step].reshape(step * 3 * GROUP, 2 * LANES)
        out[at : at + step] = three_pass(rows, table[...]).reshape(step, 3, GROUP, 2 * LANES)


def middle_kernel(spread, out, first, spectra):
    scale = 1.0 / (128.0 * 8192.0)

    def transform(number, half):
        shift = 0.5 * half
        for b in range(8):
            column = [
                turn(load_pair(spread, 8 * a + b, number), -a * shift / 8.0) for a in range(8)
            ]
            for q, value in enumerate(dft8(column, -1)):
                store_pair(first, turn(value, -b * (q + shift) / 64.0), 8 * b + q)
        for q in range(8):
            column = [load_pair(first, 8 * b + q) for b in range(8)]
            for p, value in enumerate(dft8(column, -1)):
                store_pair(spectra, value, number, q + 8 * p)

    for half in range(2):
        for number in range(3):
            transform(number, half)
        for at in range(OUTER):
            c, s = unit((2 * at + half) / 128.0)
            c, s = (1.0 + s) * scale, -c * scale
            r, i = load_pair(spectra, 2, at)
            r, i = r * c - i * s, i * c + r * s
            for number in range(2):
                fr, fi = load_pair(spectra, number, at)
                store_pair(spectra, (r * fr + i * fi, i * fr - r * fi), number, at)
        for number in range(2):
            for q in range(8):
                column = [load_pair(spectra, number, q + 8 * p) for p in range(8)]
                for b, value in enumerate(dft8(column, 1)):
                    store_pair(first, turn(value, b * q / 64.0), 8 * b + q)
            for b in range(8):
                column = [load_pair(first, 8 * b + q) for q in range(8)]
                for a, value in enumerate(dft8(column, 1)):
                    at = 8 * a + b
                    if half:
                        value = plus(load_pair(out, at, number), turn(value, at / 128.0))
                    store_pair(out, value, at, number)


def inverse_kernel(returned, phases, table, grad_signal, grad_filter, first, second):
    step = 8
    for at in range(0, OUTER, step):
        rows = returned[at : at + step].reshape(step * 2 * GROUP, 2 * LANES)
        second[at : at + step] = three_pass(rows, table[...]).reshape(step, 2, GROUP, 2 * LANES)
    for number, target in enumerate((grad_signal, grad_filter)):
        for q in range(8):
            column = []
            for p in range(8):
                at = q + 8 * p
                r, i = load_pair(second, at, number)
                c = phases[at : at + 1, :LANES]
                s = phases[at : at + 1, LANES:]
                column.append((r * c - i * s, i * c + r * s))
            for b, value in enumerate(dft8(column, 1)):
                store_pair(first, turn(value, b * (q + 0.25) / 64.0), 8 * b + q)
        for b in range(8):
            column = [load_pair(first, 8 * b + q) for q in range(8)]
            for a, (r, i) in enumerate(dft8(column, 1)):
                c, s = unit(a / 32.0)
                at = (8 * a + b) * LANES
                target[:, at : at + LANES] = r * c - i * s


def phase_table():
    turns = np.arange(LANES)[None, :] * (np.arange(OUTER)[:, None] + 0.25) / 8192.0
    angle = 2.0 * np.pi * turns
    return np.concatenate([np.cos(angle), np.sin(angle)], axis=1).astype(np.float32)


def section_table(inverse):
    angle = 2.0 * np.pi * (np.outer(np.arange(LANES), np.arange(LANES)) % LANES) / LANES
    c, s = np.cos(angle), np.sin(angle)
    whole = np.block([[c, -s], [s, c]])
    if inverse:
        whole = whole.T
    high = whole.astype(np.float32).astype(ml_dtypes.bfloat16)
    low = (whole - high.astype(np.float64)).astype(np.float32).astype(ml_dtypes.bfloat16)
    return np.concatenate([high, high, low], axis=0)


def whole_block(shape):
    return pl.BlockSpec(shape, lambda g: (0,) * len(shape))


PARAMS = pltpu.CompilerParams(vmem_limit_bytes=40 * 1024 * 1024)


def forward(signal, cotangent, long_filter):
    channels = signal.shape[0]
    rows = pl.BlockSpec((GROUP, OUTER * LANES), lambda g: (g, 0))
    return pl.pallas_call(
        forward_kernel,
        grid=(channels // GROUP,),
        in_specs=[rows] * 3 + [whole_block((OUTER, 2 * LANES)), whole_block((6 * LANES, 2 * LANES))],
        out_specs=pl.BlockSpec((OUTER, 3, GROUP, 2 * LANES), lambda g: (0, 0, g, 0)),
        out_shape=jax.ShapeDtypeStruct((OUTER, 3, channels, 2 * LANES), jnp.float32),
        scratch_shapes=[
            pltpu.VMEM((OUTER, GROUP, 2 * LANES), jnp.float32),
            pltpu.VMEM((OUTER, 3 * GROUP, 2 * LANES), jnp.float32),
        ],
        compiler_params=PARAMS,
        name="forward",
    )(signal, cotangent, long_filter, phase_table(), section_table(False))


def middle(spread):
    channels = spread.shape[2]
    return pl.pallas_call(
        middle_kernel,
        grid=(channels // GROUP,),
        in_specs=[pl.BlockSpec((OUTER, 3, GROUP, 2 * LANES), lambda g: (0, 0, g, 0))],
        out_specs=pl.BlockSpec((OUTER, 2, GROUP, 2 * LANES), lambda g: (0, 0, g, 0)),
        out_shape=jax.ShapeDtypeStruct((OUTER, 2, channels, 2 * LANES), jnp.float32),
        scratch_shapes=[
            pltpu.VMEM((OUTER, GROUP, 2 * LANES), jnp.float32),
            pltpu.VMEM((3, OUTER, GROUP, 2 * LANES), jnp.float32),
        ],
        compiler_params=PARAMS,
        name="middle",
    )(spread)


def inverse(returned):
    channels = returned.shape[2]
    rows = pl.BlockSpec((GROUP, OUTER * LANES), lambda g: (g, 0))
    result = jax.ShapeDtypeStruct((channels, OUTER * LANES), jnp.float32)
    return pl.pallas_call(
        inverse_kernel,
        grid=(channels // GROUP,),
        in_specs=[
            pl.BlockSpec((OUTER, 2, GROUP, 2 * LANES), lambda g: (0, 0, g, 0)),
            whole_block((OUTER, 2 * LANES)),
            whole_block((6 * LANES, 2 * LANES)),
        ],
        out_specs=[rows, rows],
        out_shape=[result, result],
        scratch_shapes=[
            pltpu.VMEM((OUTER, GROUP, 2 * LANES), jnp.float32),
            pltpu.VMEM((OUTER, 2, GROUP, 2 * LANES), jnp.float32),
        ],
        compiler_params=PARAMS,
        name="inverse",
    )(returned, phase_table(), section_table(True))


def exchange(blocks):
    sizes = blocks.shape
    flat = blocks.reshape(sizes[0], sizes[1] * sizes[2], sizes[3])
    moved = lax.all_to_all(flat, ("seqo", "seqi"), split_axis=0, concat_axis=0, tiled=True)
    return moved.reshape(sizes)


def on_device(signal, cotangent, long_filter):
    spread = exchange(forward(signal, cotangent, long_filter))
    grad_signal, grad_filter = inverse(exchange(middle(spread)))
    return grad_signal, grad_filter


def solution(mesh):
    spec = P("chan", ("seqo", "seqi"))
    return jax.shard_map(
        on_device, mesh=mesh, in_specs=(spec,) * 3, out_specs=(spec,) * 2, check_vma=False
    )
```

```python
import math

import jax
import jax.numpy as jnp
import ml_dtypes
import numpy as np
from jax import lax
from jax.experimental import pallas as pl
from jax.experimental.pallas import tpu as pltpu
from jax.sharding import PartitionSpec as P

LANES = 128
BLOCKS = 64
ROWS = 64
TILE = 8
TILES = ROWS // TILE
HALF_TILES = TILES // 2
LENGTH = BLOCKS * ROWS * LANES
ROOT_HALF = math.sqrt(0.5)


def unit(turns):
    return (math.cos(2.0 * math.pi * turns), math.sin(2.0 * math.pi * turns))


def plus(a, b):
    return (a[0] + b[0], a[1] + b[1])


def minus(a, b):
    return (a[0] - b[0], a[1] - b[1])


def turn(a, turns):
    turns = turns % 1.0
    if turns == 0.0:
        return a
    c, s = unit(turns)
    return (a[0] * c - a[1] * s, a[1] * c + a[0] * s)


def quarter(a, sign):
    if sign > 0:
        return (-a[1], a[0])
    return (a[1], -a[0])


def dft4(v, sign):
    t0, t1 = plus(v[0], v[2]), minus(v[0], v[2])
    t2, t3 = plus(v[1], v[3]), quarter(minus(v[1], v[3]), sign)
    return [plus(t0, t2), plus(t1, t3), minus(t0, t2), minus(t1, t3)]


def dft8(v, sign):
    up = [plus(v[n], v[n + 4]) for n in range(4)]
    down = [minus(v[n], v[n + 4]) for n in range(4)]
    r, i = down[1]
    down[1] = ((r - sign * i) * ROOT_HALF, (i + sign * r) * ROOT_HALF)
    down[2] = quarter(down[2], sign)
    r, i = down[3]
    down[3] = ((-r - sign * i) * ROOT_HALF, (sign * r - i) * ROOT_HALF)
    even, odd = dft4(up, sign), dft4(down, sign)
    return [even[k // 2] if k % 2 == 0 else odd[k // 2] for k in range(8)]


def load_pair(ref, at):
    return (ref[at, :, :LANES], ref[at, :, LANES:])


def store_pair(ref, pair, at):
    ref[at, :, :LANES] = pair[0]
    ref[at, :, LANES:] = pair[1]


def split(rows):
    high = rows.astype(jnp.bfloat16)
    return high, (rows - high.astype(jnp.float32)).astype(jnp.bfloat16)


def times_right(rows, table):
    high, low = split(rows)
    return jnp.dot(
        jnp.concatenate([high, low, high], axis=1), table, preferred_element_type=jnp.float32
    )


def times_left(table, columns):
    high, low = split(columns)
    return jnp.dot(
        table, jnp.concatenate([high, high, low], axis=0), preferred_element_type=jnp.float32
    )


def pack_kernel(signal, cotangent, long_filter, out):
    step = pl.program_id(0)

    @pl.when(step < pl.num_programs(0) - 1)
    def _():
        for u in range(TILES):
            at = slice(TILE * u, TILE * (u + 1))
            for source, core in ((long_filter, 0), (signal, 1), (cotangent, None)):
                slabs = [
                    source[:, (TILE * u + v) * LANES : (TILE * u + v + 1) * LANES]
                    for v in range(TILE)
                ]
                turned = jnp.swapaxes(jnp.stack(slabs), 0, 1)
                if core is None:
                    low = ROWS + TILE * (u % HALF_TILES)
                    out[:, u // HALF_TILES, low : low + TILE] = turned
                else:
                    out[:, core, at] = turned

    @pl.when(step == pl.num_programs(0) - 1)
    def _():
        out[...] = jnp.zeros(out.shape, out.dtype)


def unpack_kernel(landed, grad_signal, grad_filter):
    for core, target in ((0, grad_signal), (1, grad_filter)):
        for u in range(TILES):
            turned = jnp.swapaxes(landed[:, core, TILE * u : TILE * (u + 1)], 0, 1)
            for v in range(TILE):
                at = (TILE * u + v) * LANES
                target[:, at : at + LANES] = turned[v]


def correlate_kernel(
    core, own, near, far, phases, left, left_back, inner, right, right_back, out, first, spectra, back
):
    step = pl.program_id(0)

    def spread_blocks(source, number, tile):
        rows = pl.ds(pl.multiple_of(tile * TILE, TILE), TILE)
        for b in range(8):
            column = []
            for a in range(8):
                c, s = unit(-a / 32.0)
                x = source[8 * a + b]
                column.append((x * c, x * s))
            for q, value in enumerate(dft8(column, -1)):
                store_pair(first, turn(value, -b * (q + 0.25) / 64.0), 8 * b + q)
        for q in range(8):
            column = [load_pair(first, 8 * b + q) for b in range(8)]
            for p, (r, i) in enumerate(dft8(column, -1)):
                at = q + 8 * p
                c, s = load_pair(phases, at)
                spectra[at, number, rows, :LANES] = r * c + i * s
                spectra[at, number, rows, LANES:] = i * c - r * s

    @pl.when(step < TILES)
    def _():
        spread_blocks(own, 0, (step + HALF_TILES * core[0]) % TILES)

    @pl.when(step < HALF_TILES)
    def _():
        spread_blocks(near, 1, (step + HALF_TILES * core[0]) % TILES)

    @pl.when((step >= HALF_TILES) & (step < TILES))
    def _():
        spread_blocks(far, 1, (step + HALF_TILES * core[0]) % TILES)

    @pl.when(step == TILES)
    def _():
        batch = 2
        c, s = inner[:, :LANES], inner[:, LANES:]

        def body(turn_number, carry):
            base = turn_number * batch
            columns = []
            for e in range(batch):
                for number in range(2):
                    x = spectra[base + e, number]
                    columns.append(jnp.concatenate([x[:, :LANES], x[:, LANES:]], axis=0))
            y = times_left(left[...], jnp.concatenate(columns, axis=1))
            rows = []
            for n in range(2 * batch):
                r = y[:ROWS, n * LANES : (n + 1) * LANES]
                i = y[ROWS:, n * LANES : (n + 1) * LANES]
                rows.append(jnp.concatenate([r * c + i * s, i * c - r * s], axis=1))
            z = times_right(jnp.concatenate(rows, axis=0), right[...])
            rows = []
            for e in range(batch):
                f = z[2 * e * ROWS : (2 * e + 1) * ROWS]
                g = z[(2 * e + 1) * ROWS : (2 * e + 2) * ROWS]
                fr, fi, gr, gi = f[:, :LANES], f[:, LANES:], g[:, :LANES], g[:, LANES:]
                rows.append(jnp.concatenate([gr * fr + gi * fi, gi * fr - gr * fi], axis=1))
            z = times_right(jnp.concatenate(rows, axis=0), right_back[...])
            columns = []
            for e in range(batch):
                r = z[e * ROWS : (e + 1) * ROWS, :LANES]
                i = z[e * ROWS : (e + 1) * ROWS, LANES:]
                columns.append(jnp.concatenate([r * c - i * s, i * c + r * s], axis=0))
            y = times_left(left_back[...], jnp.concatenate(columns, axis=1))
            for e in range(batch):
                back[base + e, :, :LANES] = y[:ROWS, e * LANES : (e + 1) * LANES]
                back[base + e, :, LANES:] = y[ROWS:, e * LANES : (e + 1) * LANES]
            return carry

        lax.fori_loop(0, BLOCKS // batch, body, 0)

    @pl.when(step > TILES)
    def _():
        rows = pl.ds(pl.multiple_of((step - TILES - 1) * TILE, TILE), TILE)
        scale = 1.0 / LENGTH
        for q in range(8):
            column = []
            for p in range(8):
                at = q + 8 * p
                r, i = back[at, rows, :LANES], back[at, rows, LANES:]
                c, s = load_pair(phases, at)
                column.append((r * c - i * s, i * c + r * s))
            for b, value in enumerate(dft8(column, 1)):
                store_pair(first, turn(value, b * (q + 0.25) / 64.0), 8 * b + q)
        for b in range(8):
            column = [load_pair(first, 8 * b + q) for q in range(8)]
            for a, (r, i) in enumerate(dft8(column, 1)):
                c, s = unit(a / 32.0)
                out[8 * a + b] = r * (c * scale) - i * (s * scale)


def side_by_side(turns):
    angle = 2.0 * np.pi * turns
    return np.concatenate([np.cos(angle), np.sin(angle)], axis=-1).astype(np.float32)


def outer_phases():
    position = np.arange(ROWS * LANES).reshape(1, ROWS, LANES)
    return side_by_side(position * (np.arange(BLOCKS).reshape(BLOCKS, 1, 1) + 0.25) / LENGTH)


def inner_phases():
    return side_by_side(np.outer(np.arange(ROWS), np.arange(LANES)) / (ROWS * LANES))


def halves(whole):
    high = whole.astype(np.float32).astype(ml_dtypes.bfloat16)
    low = (whole - high.astype(np.float64)).astype(np.float32).astype(ml_dtypes.bfloat16)
    return high, low


def rotation(size, inverse):
    angle = 2.0 * np.pi * (np.outer(np.arange(size), np.arange(size)) % size) / size
    c, s = np.cos(angle), np.sin(angle)
    whole = np.block([[c, s], [-s, c]])
    return whole.T if inverse else whole


def left_table(inverse):
    high, low = halves(rotation(ROWS, inverse))
    return np.concatenate([high, low, high], axis=1)


def right_table(inverse):
    high, low = halves(rotation(LANES, inverse).T)
    return np.concatenate([high, high, low], axis=0)


PARAMS = pltpu.CompilerParams(vmem_limit_bytes=56 * 1024 * 1024)


def pack(signal, cotangent, long_filter, chips):
    channels = signal.shape[0]
    groups = channels // TILE
    rows = pl.BlockSpec((TILE, ROWS * LANES), lambda g: (jnp.minimum(g, groups - 1), 0))
    height = ROWS + ROWS // 2
    return pl.pallas_call(
        pack_kernel,
        grid=(chips // TILE,),
        in_specs=[rows] * 3,
        out_specs=pl.BlockSpec((TILE, 2, height, LANES), lambda g: (g, 0, 0, 0)),
        out_shape=jax.ShapeDtypeStruct((chips, 2, height, LANES), jnp.float32),
        compiler_params=PARAMS,
        name="pack",
    )(signal, cotangent, long_filter)


def unpack(landed, channels):
    rows = pl.BlockSpec((TILE, ROWS * LANES), lambda g: (g, 0))
    result = jax.ShapeDtypeStruct((channels, ROWS * LANES), jnp.float32)
    return pl.pallas_call(
        unpack_kernel,
        grid=(channels // TILE,),
        in_specs=[pl.BlockSpec((TILE, 2, ROWS, LANES), lambda g: (g, 0, 0, 0))],
        out_specs=[rows, rows],
        out_shape=[result, result],
        compiler_params=PARAMS,
        name="unpack",
    )(landed)


def correlate(core, arrived, swapped):
    last = TILES - 1

    def whole_block(table):
        return pl.BlockSpec(table.shape, lambda i, c: (0,) * table.ndim)

    def tile_of(i, c):
        return (i + HALF_TILES * c[0]) % TILES

    def phase_at(i, c):
        return (0, jnp.where(i < TILES, tile_of(i, c), jnp.maximum(i - TILES - 1, 0)), 0)

    tables = [
        left_table(False),
        left_table(True),
        inner_phases(),
        right_table(False),
        right_table(True),
    ]
    tile = (BLOCKS, TILE, LANES)
    return pl.pallas_call(
        correlate_kernel,
        grid_spec=pltpu.PrefetchScalarGridSpec(
            num_scalar_prefetch=1,
            grid=(2 * TILES + 1,),
            in_specs=[
                pl.BlockSpec(tile, lambda i, c: (0, tile_of(jnp.minimum(i, last), c), 0)),
                pl.BlockSpec(tile, lambda i, c: (0, TILES + jnp.minimum(i, HALF_TILES - 1), 0)),
                pl.BlockSpec(tile, lambda i, c: (0, jnp.clip(i - HALF_TILES, 0, HALF_TILES - 1), 0)),
                pl.BlockSpec((BLOCKS, TILE, 2 * LANES), phase_at),
            ]
            + [whole_block(table) for table in tables],
            out_specs=pl.BlockSpec(tile, lambda i, c: (0, jnp.maximum(i - TILES - 1, 0), 0)),
            scratch_shapes=[
                pltpu.VMEM((BLOCKS, TILE, 2 * LANES), jnp.float32),
                pltpu.VMEM((BLOCKS, 2, ROWS, 2 * LANES), jnp.float32),
                pltpu.VMEM((BLOCKS, ROWS, 2 * LANES), jnp.float32),
            ],
        ),
        out_shape=jax.ShapeDtypeStruct((BLOCKS, ROWS, LANES), jnp.float32),
        compiler_params=PARAMS,
        name="correlate",
    )(core, arrived, arrived, swapped, outer_phases(), *tables)


def exchange(blocks):
    return lax.all_to_all(blocks, ("seqo", "seqi"), split_axis=0, concat_axis=0, tiled=True)


def on_device(signal, cotangent, long_filter):
    channels = signal.shape[0]
    inner = lax.axis_size("seqi")
    members = lax.axis_size("seqo") * inner
    packed = pack(signal, cotangent, long_filter, members // 2)
    arrived = exchange(packed.reshape(members, *packed.shape[2:]))
    swapped = lax.ppermute(arrived[:, ROWS:], "seqi", [(n, n ^ 1) for n in range(inner)])
    core = (lax.axis_index("seqi") % 2).astype(jnp.int32).reshape(1)
    landed = exchange(correlate(core, arrived, swapped))
    return tuple(unpack(landed.reshape(members // 2, 2, ROWS, LANES), channels))


def solution(mesh):
    spec = P("chan", ("seqo", "seqi"))
    return jax.shard_map(
        on_device, mesh=mesh, in_specs=(spec,) * 3, out_specs=(spec,) * 2, check_vma=False
    )
```

```python
import math

import jax
import jax.numpy as jnp
import ml_dtypes
import numpy as np
from jax import lax
from jax.experimental import pallas as pl
from jax.experimental.pallas import tpu as pltpu
from jax.sharding import PartitionSpec as P

LANES = 128
BLOCKS = 64
ROWS = 64
TILE = 8
TILES = ROWS // TILE
HALF_TILES = TILES // 2
LENGTH = BLOCKS * ROWS * LANES
ROOT_HALF = math.sqrt(0.5)


def unit(turns):
    return (math.cos(2.0 * math.pi * turns), math.sin(2.0 * math.pi * turns))


def plus(a, b):
    return (a[0] + b[0], a[1] + b[1])


def minus(a, b):
    return (a[0] - b[0], a[1] - b[1])


def turn(a, turns):
    turns = turns % 1.0
    if turns == 0.0:
        return a
    c, s = unit(turns)
    return (a[0] * c - a[1] * s, a[1] * c + a[0] * s)


def quarter(a, sign):
    if sign > 0:
        return (-a[1], a[0])
    return (a[1], -a[0])


def dft4(v, sign):
    t0, t1 = plus(v[0], v[2]), minus(v[0], v[2])
    t2, t3 = plus(v[1], v[3]), quarter(minus(v[1], v[3]), sign)
    return [plus(t0, t2), plus(t1, t3), minus(t0, t2), minus(t1, t3)]


def dft8(v, sign):
    up = [plus(v[n], v[n + 4]) for n in range(4)]
    down = [minus(v[n], v[n + 4]) for n in range(4)]
    r, i = down[1]
    down[1] = ((r - sign * i) * ROOT_HALF, (i + sign * r) * ROOT_HALF)
    down[2] = quarter(down[2], sign)
    r, i = down[3]
    down[3] = ((-r - sign * i) * ROOT_HALF, (sign * r - i) * ROOT_HALF)
    even, odd = dft4(up, sign), dft4(down, sign)
    return [even[k // 2] if k % 2 == 0 else odd[k // 2] for k in range(8)]


def load_pair(ref, at):
    return (ref[at, :, :LANES], ref[at, :, LANES:])


def store_pair(ref, pair, at):
    ref[at, :, :LANES] = pair[0]
    ref[at, :, LANES:] = pair[1]


def split(rows):
    high = rows.astype(jnp.bfloat16)
    return high, (rows - high.astype(jnp.float32)).astype(jnp.bfloat16)


def times_right(rows, table):
    high, low = split(rows)
    return jnp.dot(
        jnp.concatenate([high, low, high], axis=1), table, preferred_element_type=jnp.float32
    )


def times_left(table, columns):
    high, low = split(columns)
    return jnp.dot(
        table, jnp.concatenate([high, high, low], axis=0), preferred_element_type=jnp.float32
    )


def pack_kernel(signal, cotangent, long_filter, out, taken, packed, in_sems, out_sems):
    groups = signal.shape[0] // TILE
    sources = (long_filter, signal, cotangent)

    def arrival(g, n):
        rows = pl.ds(TILE * g, TILE)
        return pltpu.make_async_copy(sources[n].at[rows], taken.at[g, n], in_sems.at[g, n])

    def departure(g, slot):
        return pltpu.make_async_copy(packed.at[g], out.at[pl.ds(TILE * slot, TILE)], out_sems.at[slot])

    for g in range(groups):
        for n in range(3):
            arrival(g, n).start()
    for g in range(groups):
        for n in range(3):
            arrival(g, n).wait()
        for u in range(TILES):
            for n in range(3):
                slabs = [
                    taken[g, n, :, (TILE * u + v) * LANES : (TILE * u + v + 1) * LANES]
                    for v in range(TILE)
                ]
                turned = jnp.swapaxes(jnp.stack(slabs), 0, 1)
                if n < 2:
                    packed[g, :, n, TILE * u : TILE * (u + 1)] = turned
                else:
                    low = ROWS + TILE * (u % HALF_TILES)
                    packed[g, :, u // HALF_TILES, low : low + TILE] = turned
        departure(g, g).start()
    for slot in range(groups, out.shape[0] // TILE):
        departure(groups - 1, slot).start()
    for slot in range(out.shape[0] // TILE):
        departure(min(slot, groups - 1), slot).wait()


def unpack_kernel(landed, grad_signal, grad_filter, taken, turned_out, in_sems, out_sems):
    groups = grad_signal.shape[0] // TILE
    targets = (grad_signal, grad_filter)

    def arrival(g):
        return pltpu.make_async_copy(landed.at[pl.ds(TILE * g, TILE)], taken.at[g], in_sems.at[g])

    def departure(g, n):
        rows = pl.ds(TILE * g, TILE)
        return pltpu.make_async_copy(turned_out.at[g, n], targets[n].at[rows], out_sems.at[g, n])

    for g in range(groups):
        arrival(g).start()
    for g in range(groups):
        arrival(g).wait()
        for n in range(2):
            for u in range(TILES):
                turned = jnp.swapaxes(taken[g, :, n, TILE * u : TILE * (u + 1)], 0, 1)
                for v in range(TILE):
                    at = (TILE * u + v) * LANES
                    turned_out[g, n, :, at : at + LANES] = turned[v]
            departure(g, n).start()
    for g in range(groups):
        for n in range(2):
            departure(g, n).wait()


def correlate_kernel(
    core,
    arrived,
    swapped,
    *refs,
):
    tables, out, copies = refs[:7], refs[7], refs[8:15]
    phases, lifts, left, left_back, inner, right, right_back = copies
    own, other, first, spectra, back, results, own_sems, other_sems, table_sems, out_sems = refs[15:]
    offset = HALF_TILES * core[0]

    def tile_rows(tile):
        return pl.ds(pl.multiple_of(tile * TILE, TILE), TILE)

    def own_copy(i):
        rows = tile_rows((i + offset) % TILES)
        return pltpu.make_async_copy(arrived.at[:, rows], own.at[i], own_sems.at[i])

    def other_copy(i):
        if i < HALF_TILES:
            source = arrived.at[:, pl.ds(ROWS + TILE * i, TILE)]
        else:
            source = swapped.at[:, pl.ds(TILE * (i - HALF_TILES), TILE)]
        return pltpu.make_async_copy(source, other.at[i], other_sems.at[i])

    def table_copy(n):
        return pltpu.make_async_copy(tables[n], copies[n], table_sems.at[n])

    def out_copy(i):
        return pltpu.make_async_copy(results.at[i], out.at[:, tile_rows(i)], out_sems.at[i])

    table_copy(0).start()
    table_copy(1).start()
    for i in range(TILES):
        own_copy(i).start()
        other_copy(i).start()
    for n in range(2, 7):
        table_copy(n).start()

    def lift(a, tile, at, sign):
        c, s = lifts[tile, at : at + 1, :LANES], lifts[tile, at : at + 1, LANES:]
        if sign > 0:
            return (a[0] * c - a[1] * s, a[1] * c + a[0] * s)
        return (a[0] * c + a[1] * s, a[1] * c - a[0] * s)

    def spread_blocks(source, i, number):
        tile = (i + offset) % TILES
        rows = tile_rows(tile)
        for b in range(8):
            column = []
            for a in range(8):
                c, s = unit(-a / 32.0)
                x = source[i, 8 * a + b]
                column.append((x * c, x * s))
            for q, value in enumerate(dft8(column, -1)):
                store_pair(first, turn(value, -b * (q + 0.25) / 64.0), 8 * b + q)
        for q in range(8):
            column = [load_pair(first, 8 * b + q) for b in range(8)]
            for p, value in enumerate(dft8(column, -1)):
                at = q + 8 * p
                r, i_part = lift(value, tile, at, -1)
                c, s = load_pair(phases, at)
                spectra[at, number, rows, :LANES] = r * c + i_part * s
                spectra[at, number, rows, LANES:] = i_part * c - r * s

    table_copy(0).wait()
    table_copy(1).wait()

    def spread_step(i, carry):
        pltpu.make_async_copy(arrived.at[:, pl.ds(0, TILE)], own.at[i], own_sems.at[i]).wait()
        pltpu.make_async_copy(arrived.at[:, pl.ds(0, TILE)], other.at[i], other_sems.at[i]).wait()
        spread_blocks(own, i, 0)
        spread_blocks(other, i, 1)
        return carry

    lax.fori_loop(0, TILES, spread_step, 0)
    for n in range(2, 7):
        table_copy(n).wait()

    batch = 16
    c, s = inner[:, :LANES], inner[:, LANES:]

    def body(turn_number, carry):
        base = turn_number * batch
        columns = []
        for e in range(batch):
            for number in range(2):
                x = spectra[base + e, number]
                columns.append(jnp.concatenate([x[:, :LANES], x[:, LANES:]], axis=0))
        y = times_left(left[...], jnp.concatenate(columns, axis=1))
        rows = []
        for n in range(2 * batch):
            r = y[:ROWS, n * LANES : (n + 1) * LANES]
            i = y[ROWS:, n * LANES : (n + 1) * LANES]
            rows.append(jnp.concatenate([r * c + i * s, i * c - r * s], axis=1))
        z = times_right(jnp.concatenate(rows, axis=0), right[...])
        rows = []
        for e in range(batch):
            f = z[2 * e * ROWS : (2 * e + 1) * ROWS]
            g = z[(2 * e + 1) * ROWS : (2 * e + 2) * ROWS]
            fr, fi, gr, gi = f[:, :LANES], f[:, LANES:], g[:, :LANES], g[:, LANES:]
            rows.append(jnp.concatenate([gr * fr + gi * fi, gi * fr - gr * fi], axis=1))
        z = times_right(jnp.concatenate(rows, axis=0), right_back[...])
        columns = []
        for e in range(batch):
            r = z[e * ROWS : (e + 1) * ROWS, :LANES]
            i = z[e * ROWS : (e + 1) * ROWS, LANES:]
            columns.append(jnp.concatenate([r * c - i * s, i * c + r * s], axis=0))
        y = times_left(left_back[...], jnp.concatenate(columns, axis=1))
        for e in range(batch):
            back[base + e, :, :LANES] = y[:ROWS, e * LANES : (e + 1) * LANES]
            back[base + e, :, LANES:] = y[ROWS:, e * LANES : (e + 1) * LANES]
        return carry

    lax.fori_loop(0, BLOCKS // batch, body, 0)

    def gather_step(tile, carry):
        rows = tile_rows(tile)
        scale = 1.0 / LENGTH
        for q in range(8):
            column = []
            for p in range(8):
                at = q + 8 * p
                r, i = back[at, rows, :LANES], back[at, rows, LANES:]
                c, s = load_pair(phases, at)
                column.append(lift((r * c - i * s, i * c + r * s), tile, at, 1))
            for b, value in enumerate(dft8(column, 1)):
                store_pair(first, turn(value, b * (q + 0.25) / 64.0), 8 * b + q)
        for b in range(8):
            column = [load_pair(first, 8 * b + q) for q in range(8)]
            for a, (r, i) in enumerate(dft8(column, 1)):
                c, s = unit(a / 32.0)
                results[tile, 8 * a + b] = r * (c * scale) - i * (s * scale)
        out_copy(tile).start()
        return carry

    lax.fori_loop(0, TILES, gather_step, 0)
    for i in range(TILES):
        out_copy(i).wait()


def side_by_side(turns):
    angle = 2.0 * np.pi * turns
    return np.concatenate([np.cos(angle), np.sin(angle)], axis=-1).astype(np.float32)


def outer_phases():
    position = np.arange(TILE * LANES).reshape(1, TILE, LANES)
    return side_by_side(position * (np.arange(BLOCKS).reshape(BLOCKS, 1, 1) + 0.25) / LENGTH)


def tile_phases():
    start = TILE * LANES * np.arange(TILES).reshape(TILES, 1, 1)
    turns = start * (np.arange(BLOCKS).reshape(1, BLOCKS, 1) + 0.25) / LENGTH
    return side_by_side(np.broadcast_to(turns, (TILES, BLOCKS, LANES)))


def inner_phases():
    return side_by_side(np.outer(np.arange(ROWS), np.arange(LANES)) / (ROWS * LANES))


def halves(whole):
    high = whole.astype(np.float32).astype(ml_dtypes.bfloat16)
    low = (whole - high.astype(np.float64)).astype(np.float32).astype(ml_dtypes.bfloat16)
    return high, low


def rotation(size, inverse):
    angle = 2.0 * np.pi * (np.outer(np.arange(size), np.arange(size)) % size) / size
    c, s = np.cos(angle), np.sin(angle)
    whole = np.block([[c, s], [-s, c]])
    return whole.T if inverse else whole


def left_table(inverse):
    high, low = halves(rotation(ROWS, inverse))
    return np.concatenate([high, low, high], axis=1)


def right_table(inverse):
    high, low = halves(rotation(LANES, inverse).T)
    return np.concatenate([high, high, low], axis=0)


PARAMS = pltpu.CompilerParams(vmem_limit_bytes=56 * 1024 * 1024)


ANY = pl.BlockSpec(memory_space=pl.ANY)


def pack(signal, cotangent, long_filter, chips):
    groups = signal.shape[0] // TILE
    height = ROWS + ROWS // 2
    return pl.pallas_call(
        pack_kernel,
        in_specs=[ANY] * 3,
        out_specs=ANY,
        out_shape=jax.ShapeDtypeStruct((chips, 2, height, LANES), jnp.float32),
        scratch_shapes=[
            pltpu.VMEM((groups, 3, TILE, ROWS * LANES), jnp.float32),
            pltpu.VMEM((groups, TILE, 2, height, LANES), jnp.float32),
            pltpu.SemaphoreType.DMA((groups, 3)),
            pltpu.SemaphoreType.DMA((chips // TILE,)),
        ],
        compiler_params=PARAMS,
        name="pack",
    )(signal, cotangent, long_filter)


def unpack(landed, channels):
    groups = channels // TILE
    result = jax.ShapeDtypeStruct((channels, ROWS * LANES), jnp.float32)
    return pl.pallas_call(
        unpack_kernel,
        in_specs=[ANY],
        out_specs=[ANY, ANY],
        out_shape=[result, result],
        scratch_shapes=[
            pltpu.VMEM((groups, TILE, 2, ROWS, LANES), jnp.float32),
            pltpu.VMEM((groups, 2, TILE, ROWS * LANES), jnp.float32),
            pltpu.SemaphoreType.DMA((groups,)),
            pltpu.SemaphoreType.DMA((groups, 2)),
        ],
        compiler_params=PARAMS,
        name="unpack",
    )(landed)


def correlate(core, arrived, swapped):
    tables = [
        outer_phases(),
        tile_phases(),
        left_table(False),
        left_table(True),
        inner_phases(),
        right_table(False),
        right_table(True),
    ]
    tile = (TILES, BLOCKS, TILE, LANES)
    return pl.pallas_call(
        correlate_kernel,
        in_specs=[pl.BlockSpec(memory_space=pltpu.SMEM)] + [ANY] * (2 + len(tables)),
        out_specs=ANY,
        out_shape=jax.ShapeDtypeStruct((BLOCKS, ROWS, LANES), jnp.float32),
        scratch_shapes=[pltpu.VMEM(table.shape, table.dtype) for table in tables]
        + [
            pltpu.VMEM(tile, jnp.float32),
            pltpu.VMEM(tile, jnp.float32),
            pltpu.VMEM((BLOCKS, TILE, 2 * LANES), jnp.float32),
            pltpu.VMEM((BLOCKS, 2, ROWS, 2 * LANES), jnp.float32),
            pltpu.VMEM((BLOCKS, ROWS, 2 * LANES), jnp.float32),
            pltpu.VMEM(tile, jnp.float32),
            pltpu.SemaphoreType.DMA((TILES,)),
            pltpu.SemaphoreType.DMA((TILES,)),
            pltpu.SemaphoreType.DMA((len(tables),)),
            pltpu.SemaphoreType.DMA((TILES,)),
        ],
        compiler_params=PARAMS,
        name="correlate",
    )(core, arrived, swapped, *tables)


def exchange(blocks):
    return lax.all_to_all(blocks, ("seqo", "seqi"), split_axis=0, concat_axis=0, tiled=True)


def on_device(signal, cotangent, long_filter):
    channels = signal.shape[0]
    inner = lax.axis_size("seqi")
    members = lax.axis_size("seqo") * inner
    packed = pack(signal, cotangent, long_filter, members // 2)
    arrived = exchange(packed.reshape(members, *packed.shape[2:]))
    swapped = lax.ppermute(arrived[:, ROWS:], "seqi", [(n, n ^ 1) for n in range(inner)])
    core = (lax.axis_index("seqi") % 2).astype(jnp.int32).reshape(1)
    landed = exchange(correlate(core, arrived, swapped))
    return tuple(unpack(landed.reshape(members // 2, 2, ROWS, LANES), channels))


def solution(mesh):
    spec = P("chan", ("seqo", "seqi"))
    return jax.shard_map(
        on_device, mesh=mesh, in_specs=(spec,) * 3, out_specs=(spec,) * 2, check_vma=False
    )
```

```python
import math

import jax
import jax.numpy as jnp
import ml_dtypes
import numpy as np
from jax import lax
from jax.experimental import pallas as pl
from jax.experimental.pallas import tpu as pltpu
from jax.sharding import PartitionSpec as P

LANES = 128
BLOCKS = 64
ROWS = 64
TILE = 8
TILES = ROWS // TILE
HALF_TILES = TILES // 2
SIZE = 4
STEPS = 8 // SIZE
LENGTH = BLOCKS * ROWS * LANES
ROOT_HALF = math.sqrt(0.5)


def unit(turns):
    return (math.cos(2.0 * math.pi * turns), math.sin(2.0 * math.pi * turns))


def plus(a, b):
    return (a[0] + b[0], a[1] + b[1])


def minus(a, b):
    return (a[0] - b[0], a[1] - b[1])


def turn(a, turns):
    turns = turns % 1.0
    if turns == 0.0:
        return a
    c, s = unit(turns)
    return (a[0] * c - a[1] * s, a[1] * c + a[0] * s)


def quarter(a, sign):
    if sign > 0:
        return (-a[1], a[0])
    return (a[1], -a[0])


def dft4(v, sign):
    t0, t1 = plus(v[0], v[2]), minus(v[0], v[2])
    t2, t3 = plus(v[1], v[3]), quarter(minus(v[1], v[3]), sign)
    return [plus(t0, t2), plus(t1, t3), minus(t0, t2), minus(t1, t3)]


def dft8(v, sign):
    up = [plus(v[n], v[n + 4]) for n in range(4)]
    down = [minus(v[n], v[n + 4]) for n in range(4)]
    r, i = down[1]
    down[1] = ((r - sign * i) * ROOT_HALF, (i + sign * r) * ROOT_HALF)
    down[2] = quarter(down[2], sign)
    r, i = down[3]
    down[3] = ((-r - sign * i) * ROOT_HALF, (sign * r - i) * ROOT_HALF)
    even, odd = dft4(up, sign), dft4(down, sign)
    return [even[k // 2] if k % 2 == 0 else odd[k // 2] for k in range(8)]


def split(rows):
    high = rows.astype(jnp.bfloat16)
    return high, (rows - high.astype(jnp.float32)).astype(jnp.bfloat16)


def times_right(rows, table):
    high, low = split(rows)
    return jnp.dot(
        jnp.concatenate([high, low, high], axis=1), table, preferred_element_type=jnp.float32
    )


def times_left(table, columns):
    high, low = split(columns)
    both = jnp.dot(
        table, jnp.concatenate([high, low], axis=0), preferred_element_type=jnp.float32
    )
    return both[: 2 * ROWS] + both[2 * ROWS :]


def pack_kernel(signal, cotangent, long_filter, out, taken, packed, in_sems, out_sems):
    groups = signal.shape[0] // TILE
    sources = (long_filter, signal, cotangent)

    def arrival(g, n):
        rows = pl.ds(TILE * g, TILE)
        return pltpu.make_async_copy(sources[n].at[rows], taken.at[g, n], in_sems.at[g, n])

    def departure(g, slot):
        return pltpu.make_async_copy(packed.at[g], out.at[pl.ds(TILE * slot, TILE)], out_sems.at[slot])

    for g in range(groups):
        for n in range(3):
            arrival(g, n).start()
    for g in range(groups):
        for n in range(3):
            arrival(g, n).wait()
        for u in range(TILES):
            for n in range(3):
                slabs = [
                    taken[g, n, :, (TILE * u + v) * LANES : (TILE * u + v + 1) * LANES]
                    for v in range(TILE)
                ]
                turned = jnp.swapaxes(jnp.stack(slabs), 0, 1)
                if n < 2:
                    packed[g, :, n, TILE * u : TILE * (u + 1)] = turned
                else:
                    low = ROWS + TILE * (u % HALF_TILES)
                    packed[g, :, u // HALF_TILES, low : low + TILE] = turned
        departure(g, g).start()
    for slot in range(groups, out.shape[0] // TILE):
        departure(groups - 1, slot).start()
    for slot in range(out.shape[0] // TILE):
        departure(min(slot, groups - 1), slot).wait()


def unpack_kernel(landed, grad_signal, grad_filter, taken, turned_out, in_sems, out_sems):
    groups = grad_signal.shape[0] // TILE
    targets = (grad_signal, grad_filter)

    def arrival(g):
        return pltpu.make_async_copy(landed.at[pl.ds(TILE * g, TILE)], taken.at[g], in_sems.at[g])

    def departure(g, n):
        rows = pl.ds(TILE * g, TILE)
        return pltpu.make_async_copy(turned_out.at[g, n], targets[n].at[rows], out_sems.at[g, n])

    for g in range(groups):
        arrival(g).start()
    for g in range(groups):
        arrival(g).wait()
        for n in range(2):
            for u in range(TILES):
                turned = jnp.swapaxes(taken[g, :, n, TILE * u : TILE * (u + 1)], 0, 1)
                for v in range(TILE):
                    at = (TILE * u + v) * LANES
                    turned_out[g, n, :, at : at + LANES] = turned[v]
            departure(g, n).start()
    for g in range(groups):
        for n in range(2):
            departure(g, n).wait()


def correlate_kernel(core, arrived, swapped, *refs):
    tables, out, copies = refs[:4], refs[4], refs[5:9]
    phases, left, inner, right = copies
    own, other, spread, even, odd, even_back, odd_back, gathered, results = refs[9:18]
    held_entered, held_multiplied, held_turned = refs[18:21]
    own_sems, other_sems, table_sems, phase_sems, out_sems = refs[21:]
    offset = HALF_TILES * core[0]

    def tile_rows(tile):
        if isinstance(tile, int):
            return slice(tile * TILE, (tile + 1) * TILE)
        return pl.ds(pl.multiple_of(tile * TILE, TILE), TILE)

    def own_copy(i):
        return pltpu.make_async_copy(arrived.at[:, pl.ds(TILE * i, TILE)], own.at[i], own_sems.at[i])

    def other_copy(i):
        if i < HALF_TILES:
            source = arrived.at[:, pl.ds(ROWS + TILE * i, TILE)]
        else:
            source = swapped.at[:, pl.ds(TILE * (i - HALF_TILES), TILE)]
        return pltpu.make_async_copy(source, other.at[(i + offset) % TILES], other_sems.at[i])

    def table_copy(n):
        return pltpu.make_async_copy(tables[n], copies[n], table_sems.at[n])

    def phase_copy(q):
        return pltpu.make_async_copy(tables[0].at[q], phases.at[q], phase_sems.at[q])

    def out_copy(i):
        return pltpu.make_async_copy(results.at[i], out.at[:, tile_rows(i)], out_sems.at[i])

    for i in range(TILES):
        own_copy(i).start()
        other_copy(i).start()
    for n in range(1, len(tables)):
        table_copy(n).start()
    for q in range(8):
        phase_copy(q).start()
    for ref in (held_entered, held_multiplied, held_turned, even_back, odd_back):
        ref[...] = jnp.zeros(ref.shape, ref.dtype)

    def over_high(source, slot, number):
        for b in range(8):
            column = []
            for a in range(8):
                c, s = unit(-a / 32.0)
                x = source[slot, 8 * a + b]
                column.append((x * c, x * s))
            for q, value in enumerate(dft8(column, -1)):
                r, i = turn(value, -b * (q + 0.25) / 64.0)
                spread[number, slot, 8 * b + q, :, :LANES] = r
                spread[number, slot, 8 * b + q, :, LANES:] = i

    def spread_step(i, carry):
        slot = (i + offset) % TILES
        pltpu.make_async_copy(arrived.at[:, pl.ds(0, TILE)], own.at[i], own_sems.at[i]).wait()
        over_high(own, i, 0)
        pltpu.make_async_copy(arrived.at[:, pl.ds(0, TILE)], other.at[slot], other_sems.at[i]).wait()
        over_high(other, slot, 1)
        return carry

    lax.fori_loop(0, TILES, spread_step, 0)
    for n in range(1, len(tables)):
        table_copy(n).wait()
    phase_copy(0).wait()

    def over_low(q, tile, number, target):
        rows = tile_rows(tile)
        column = []
        for b in range(8):
            at = 8 * b + q
            column.append((spread[number, tile, at, :, :LANES], spread[number, tile, at, :, LANES:]))
        for p, (r, i) in enumerate(dft8(column, -1)):
            c, s = phases[q, p, rows, :LANES], phases[q, p, rows, LANES:]
            target[p, number, rows, :LANES] = r * c + i * s
            target[p, number, rows, LANES:] = i * c - r * s

    def back_low(q, tile, source):
        rows = tile_rows(tile)
        column = []
        for p in range(8):
            r, i = source[p, rows, :LANES], source[p, rows, LANES:]
            c, s = phases[q, p, rows, :LANES], phases[q, p, rows, LANES:]
            column.append((r * c - i * s, i * c + r * s))
        for b, (r, i) in enumerate(dft8(column, 1)):
            gathered[tile, 8 * b + q, :, :LANES] = r
            gathered[tile, 8 * b + q, :, LANES:] = i

    c_inner, s_inner = inner[:, :LANES], inner[:, LANES:]

    def entry_columns(source, first_bin):
        columns = []
        for e in range(SIZE):
            for number in range(2):
                x = source[first_bin + e, number]
                columns.append(jnp.concatenate([x[:, :LANES], x[:, LANES:]], axis=0))
        return columns

    def lanes(y, n):
        at = slice(n * LANES, (n + 1) * LANES)
        return y[:ROWS, at], y[ROWS:, at]

    def entry_rows(y):
        rows = []
        for n in range(2 * SIZE):
            r, i = lanes(y, n)
            rows.append(
                jnp.concatenate(
                    [r * c_inner + i * s_inner, i * c_inner - r * s_inner], axis=1
                )
            )
        return jnp.concatenate(rows, axis=0)

    def product_rows(z):
        made = []
        for e in range(SIZE):
            f = z[2 * e * ROWS : (2 * e + 1) * ROWS]
            g = z[(2 * e + 1) * ROWS : (2 * e + 2) * ROWS]
            fr, fi, gr, gi = f[:, :LANES], f[:, LANES:], g[:, :LANES], g[:, LANES:]
            made.append(jnp.concatenate([gi * fr - gr * fi, gr * fr + gi * fi], axis=1))
        return jnp.concatenate(made, axis=0)

    def exit_columns(z):
        columns = []
        for e in range(SIZE):
            i = z[e * ROWS : (e + 1) * ROWS, :LANES]
            r = z[e * ROWS : (e + 1) * ROWS, LANES:]
            columns.append(
                jnp.concatenate(
                    [i * c_inner + r * s_inner, r * c_inner - i * s_inner], axis=0
                )
            )
        return jnp.concatenate(columns, axis=1)

    def leave(target, first_bin, y, start):
        for e in range(SIZE):
            i, r = lanes(y, start + e)
            target[first_bin + e, :, :LANES] = r
            target[first_bin + e, :, LANES:] = i

    def advance(flight, source, first_bin, target, last_bin):
        entered, multiplied, turned = flight
        leave(target, last_bin, times_left(left[...], turned), 0)
        turned = exit_columns(times_right(multiplied, right[...]))
        multiplied = product_rows(times_right(entered, right[...]))
        if source is not None:
            columns = jnp.concatenate(entry_columns(source, first_bin), axis=1)
            entered = entry_rows(times_left(left[...], columns))
        return entered, multiplied, turned

    def left_at(step):
        return -((step - 3) // STEPS), (step - 3) % STEPS * SIZE

    delay = next(ago for ago, at in map(left_at, range(STEPS)) if at + SIZE == 8)

    def half(flight, now, q_next, then, q_last, backs):
        per_step = 2 * TILES // STEPS
        for step in range(STEPS):
            ago, last_bin = left_at(step)
            flight = advance(flight, now, step * SIZE, backs[ago % 2], last_bin)
            for n in range(step * per_step, (step + 1) * per_step):
                over_low(q_next, n // 2, n % 2, then)
            if last_bin + SIZE == 8:
                for tile in range(TILES):
                    back_low(q_last, tile, backs[ago % 2])
        return flight

    for tile in range(TILES):
        over_low(0, tile, 0, even)
        over_low(0, tile, 1, even)

    def pair_step(t, carry):
        phase_copy(2 * t + 1).wait()

        @pl.when(t < 3)
        def _():
            phase_copy(2 * t + 2).wait()

        flight = held_entered[...], held_multiplied[...], held_turned[...]
        last = jnp.maximum(2 * t - delay, 0)
        flight = half(flight, even, 2 * t + 1, odd, last, (even_back, odd_back))
        last = jnp.maximum(2 * t + 1 - delay, 0)
        flight = half(flight, odd, jnp.minimum(2 * t + 2, 7), even, last, (odd_back, even_back))
        held_entered[...], held_multiplied[...], held_turned[...] = flight
        return carry

    lax.fori_loop(0, 4, pair_step, 0)
    flight = held_entered[...], held_multiplied[...], held_turned[...]
    for step in range(3):
        ago, last_bin = left_at(step)
        q = 8 - ago
        target = (even_back, odd_back)[q % 2]
        flight = advance(flight, None, 0, target, last_bin)
        if last_bin + SIZE == 8:
            for tile in range(TILES):
                back_low(q, tile, target)

    def gather_step(tile, carry):
        scale = 1.0 / LENGTH
        for b in range(8):
            column = []
            for q in range(8):
                at = 8 * b + q
                value = (gathered[tile, at, :, :LANES], gathered[tile, at, :, LANES:])
                column.append(turn(value, b * (q + 0.25) / 64.0))
            for a, (r, i) in enumerate(dft8(column, 1)):
                c, s = unit(a / 32.0)
                results[tile, 8 * a + b] = r * (c * scale) - i * (s * scale)
        out_copy(tile).start()
        return carry

    lax.fori_loop(0, TILES, gather_step, 0)
    for i in range(TILES):
        out_copy(i).wait()


def side_by_side(turns):
    angle = 2.0 * np.pi * turns
    return np.concatenate([np.cos(angle), np.sin(angle)], axis=-1).astype(np.float32)


def outer_phases():
    position = np.arange(ROWS * LANES).reshape(1, ROWS, LANES)
    bins = np.arange(BLOCKS).reshape(8, 8).T.reshape(BLOCKS, 1, 1)
    turns = side_by_side(position * (bins + 0.25) / LENGTH)
    return turns.reshape(8, 8, ROWS, 2 * LANES)


def inner_phases():
    return side_by_side(np.outer(np.arange(ROWS), np.arange(LANES)) / (ROWS * LANES))


def halves(whole):
    high = whole.astype(np.float32).astype(ml_dtypes.bfloat16)
    low = (whole - high.astype(np.float64)).astype(np.float32).astype(ml_dtypes.bfloat16)
    return high, low


def rotation(size):
    angle = 2.0 * np.pi * (np.outer(np.arange(size), np.arange(size)) % size) / size
    c, s = np.cos(angle), np.sin(angle)
    return np.block([[c, s], [-s, c]])


def left_table():
    high, low = halves(rotation(ROWS))
    return np.block([[high, high], [low, np.zeros_like(low)]])


def right_table():
    high, low = halves(rotation(LANES).T)
    return np.concatenate([high, high, low], axis=0)


PARAMS = pltpu.CompilerParams(vmem_limit_bytes=56 * 1024 * 1024)


ANY = pl.BlockSpec(memory_space=pl.ANY)


def pack(signal, cotangent, long_filter, chips):
    groups = signal.shape[0] // TILE
    height = ROWS + ROWS // 2
    return pl.pallas_call(
        pack_kernel,
        in_specs=[ANY] * 3,
        out_specs=ANY,
        out_shape=jax.ShapeDtypeStruct((chips, 2, height, LANES), jnp.float32),
        scratch_shapes=[
            pltpu.VMEM((groups, 3, TILE, ROWS * LANES), jnp.float32),
            pltpu.VMEM((groups, TILE, 2, height, LANES), jnp.float32),
            pltpu.SemaphoreType.DMA((groups, 3)),
            pltpu.SemaphoreType.DMA((chips // TILE,)),
        ],
        compiler_params=PARAMS,
        name="pack",
    )(signal, cotangent, long_filter)


def unpack(landed, channels):
    groups = channels // TILE
    result = jax.ShapeDtypeStruct((channels, ROWS * LANES), jnp.float32)
    return pl.pallas_call(
        unpack_kernel,
        in_specs=[ANY],
        out_specs=[ANY, ANY],
        out_shape=[result, result],
        scratch_shapes=[
            pltpu.VMEM((groups, TILE, 2, ROWS, LANES), jnp.float32),
            pltpu.VMEM((groups, 2, TILE, ROWS * LANES), jnp.float32),
            pltpu.SemaphoreType.DMA((groups,)),
            pltpu.SemaphoreType.DMA((groups, 2)),
        ],
        compiler_params=PARAMS,
        name="unpack",
    )(landed)


def correlate(core, arrived, swapped):
    tables = [
        outer_phases(),
        left_table(),
        inner_phases(),
        right_table(),
    ]
    tile = (TILES, BLOCKS, TILE, LANES)
    return pl.pallas_call(
        correlate_kernel,
        in_specs=[pl.BlockSpec(memory_space=pltpu.SMEM)] + [ANY] * (2 + len(tables)),
        out_specs=ANY,
        out_shape=jax.ShapeDtypeStruct((BLOCKS, ROWS, LANES), jnp.float32),
        scratch_shapes=[pltpu.VMEM(table.shape, table.dtype) for table in tables]
        + [
            pltpu.VMEM(tile, jnp.float32),
            pltpu.VMEM(tile, jnp.float32),
            pltpu.VMEM((2, TILES, BLOCKS, TILE, 2 * LANES), jnp.float32),
            pltpu.VMEM((8, 2, ROWS, 2 * LANES), jnp.float32),
            pltpu.VMEM((8, 2, ROWS, 2 * LANES), jnp.float32),
            pltpu.VMEM((8, ROWS, 2 * LANES), jnp.float32),
            pltpu.VMEM((8, ROWS, 2 * LANES), jnp.float32),
            pltpu.VMEM((TILES, BLOCKS, TILE, 2 * LANES), jnp.float32),
            pltpu.VMEM(tile, jnp.float32),
            pltpu.VMEM((2 * SIZE * ROWS, 2 * LANES), jnp.float32),
            pltpu.VMEM((SIZE * ROWS, 2 * LANES), jnp.float32),
            pltpu.VMEM((2 * ROWS, SIZE * LANES), jnp.float32),
            pltpu.SemaphoreType.DMA((TILES,)),
            pltpu.SemaphoreType.DMA((TILES,)),
            pltpu.SemaphoreType.DMA((len(tables),)),
            pltpu.SemaphoreType.DMA((8,)),
            pltpu.SemaphoreType.DMA((TILES,)),
        ],
        compiler_params=PARAMS,
        name="correlate",
    )(core, arrived, swapped, *tables)


def exchange(blocks):
    return lax.all_to_all(blocks, ("seqo", "seqi"), split_axis=0, concat_axis=0, tiled=True)


def on_device(signal, cotangent, long_filter):
    channels = signal.shape[0]
    inner = lax.axis_size("seqi")
    members = lax.axis_size("seqo") * inner
    packed = pack(signal, cotangent, long_filter, members // 2)
    arrived = exchange(packed.reshape(members, *packed.shape[2:]))
    swapped = lax.ppermute(arrived[:, ROWS:], "seqi", [(n, n ^ 1) for n in range(inner)])
    core = (lax.axis_index("seqi") % 2).astype(jnp.int32).reshape(1)
    landed = exchange(correlate(core, arrived, swapped))
    return tuple(unpack(landed.reshape(members // 2, 2, ROWS, LANES), channels))


def solution(mesh):
    spec = P("chan", ("seqo", "seqi"))
    return jax.shard_map(
        on_device, mesh=mesh, in_specs=(spec,) * 3, out_specs=(spec,) * 2, check_vma=False
    )
```

```python
import math

import jax
import jax.numpy as jnp
import ml_dtypes
import numpy as np
from jax import lax
from jax.experimental import pallas as pl
from jax.experimental.pallas import tpu as pltpu
from jax.sharding import Mesh, PartitionSpec as P

LANES = 128
BLOCKS = 64
ROWS = 64
TILE = 8
TILES = ROWS // TILE
HALF_TILES = TILES // 2
SIZE = 4
STEPS = 8 // SIZE
LENGTH = BLOCKS * ROWS * LANES
SEQUENCE = ("z", "y", "xh", "core")
LISTED = ("core", "z", "xh", "y")
ROOT_HALF = math.sqrt(0.5)


def slot_of(block):
    z, y, xh, core = block // 16, block // 4 % 4, block // 2 % 2, block % 2
    return 32 * core + 8 * z + 4 * xh + y


def unit(turns):
    return (math.cos(2.0 * math.pi * turns), math.sin(2.0 * math.pi * turns))


def plus(a, b):
    return (a[0] + b[0], a[1] + b[1])


def minus(a, b):
    return (a[0] - b[0], a[1] - b[1])


def turn(a, turns):
    turns = turns % 1.0
    if turns == 0.0:
        return a
    c, s = unit(turns)
    return (a[0] * c - a[1] * s, a[1] * c + a[0] * s)


def quarter(a, sign):
    if sign > 0:
        return (-a[1], a[0])
    return (a[1], -a[0])


def dft4(v, sign):
    t0, t1 = plus(v[0], v[2]), minus(v[0], v[2])
    t2, t3 = plus(v[1], v[3]), quarter(minus(v[1], v[3]), sign)
    return [plus(t0, t2), plus(t1, t3), minus(t0, t2), minus(t1, t3)]


def dft8(v, sign):
    up = [plus(v[n], v[n + 4]) for n in range(4)]
    down = [minus(v[n], v[n + 4]) for n in range(4)]
    r, i = down[1]
    down[1] = ((r - sign * i) * ROOT_HALF, (i + sign * r) * ROOT_HALF)
    down[2] = quarter(down[2], sign)
    r, i = down[3]
    down[3] = ((-r - sign * i) * ROOT_HALF, (sign * r - i) * ROOT_HALF)
    even, odd = dft4(up, sign), dft4(down, sign)
    return [even[k // 2] if k % 2 == 0 else odd[k // 2] for k in range(8)]


def split(rows):
    high = rows.astype(jnp.bfloat16)
    return high, (rows - high.astype(jnp.float32)).astype(jnp.bfloat16)


def times_right(rows, table):
    high, low = split(rows)
    return jnp.dot(
        jnp.concatenate([high, low, high], axis=1), table, preferred_element_type=jnp.float32
    )


def times_left(table, columns):
    high, low = split(columns)
    both = jnp.dot(
        table, jnp.concatenate([high, low], axis=0), preferred_element_type=jnp.float32
    )
    return both[: 2 * ROWS] + both[2 * ROWS :]


def pack_kernel(signal, cotangent, long_filter, out, taken, packed, in_sems, out_sems):
    groups = signal.shape[0] // TILE
    slots = out.shape[1] // TILE
    sources = (long_filter, signal, cotangent)

    def arrival(g, n):
        rows = pl.ds(TILE * g, TILE)
        return pltpu.make_async_copy(sources[n].at[rows], taken.at[g, n], in_sems.at[g, n])

    def departure(slot, n):
        g = min(slot, groups - 1)
        chips = pl.ds(TILE * slot, TILE)
        if n < 2:
            rows = pl.ds(0, ROWS)
            source, target = packed.at[g, n, :, rows], out.at[n, chips, rows]
        else:
            rows = pl.ds(ROWS, ROWS // 2)
            source, target = packed.at[g, :, :, rows], out.at[:, chips, rows]
        return pltpu.make_async_copy(source, target, out_sems.at[slot, n])

    for g in range(groups):
        for n in range(3):
            arrival(g, n).start()
    for g in range(groups):
        for n in range(3):
            arrival(g, n).wait()
            for u in range(TILES):
                slabs = [
                    taken[g, n, :, (TILE * u + v) * LANES : (TILE * u + v + 1) * LANES]
                    for v in range(TILE)
                ]
                turned = jnp.swapaxes(jnp.stack(slabs), 0, 1)
                if n < 2:
                    packed[g, n, :, TILE * u : TILE * (u + 1)] = turned
                else:
                    low = ROWS + TILE * (u % HALF_TILES)
                    packed[g, u // HALF_TILES, :, low : low + TILE] = turned
            departure(g, n).start()
    for slot in range(groups, slots):
        for n in range(3):
            departure(slot, n).start()
    for slot in range(slots):
        for n in range(3):
            departure(slot, n).wait()


def unpack_kernel(landed, grad_signal, grad_filter, taken, turned_out, in_sems, out_sems):
    groups = grad_signal.shape[0] // TILE
    targets = (grad_signal, grad_filter)

    def arrival(g, n):
        chips = pl.ds(TILE * g, TILE)
        return pltpu.make_async_copy(landed.at[n, chips], taken.at[g, n], in_sems.at[g, n])

    def departure(g, n):
        rows = pl.ds(TILE * g, TILE)
        return pltpu.make_async_copy(turned_out.at[g, n], targets[n].at[rows], out_sems.at[g, n])

    for g in range(groups):
        for n in range(2):
            arrival(g, n).start()
    for g in range(groups):
        for n in range(2):
            arrival(g, n).wait()
            for u in range(TILES):
                turned = jnp.swapaxes(taken[g, n, :, TILE * u : TILE * (u + 1)], 0, 1)
                for v in range(TILE):
                    at = (TILE * u + v) * LANES
                    turned_out[g, n, :, at : at + LANES] = turned[v]
            departure(g, n).start()
    for g in range(groups):
        for n in range(2):
            departure(g, n).wait()


def correlate_kernel(core, arrived, swapped, *refs):
    tables, out, copies = refs[:4], refs[4], refs[5:9]
    phases, left, inner, right = copies
    own, other, spread, even, odd, even_back, odd_back, gathered, results = refs[9:18]
    held_entered, held_multiplied, held_turned = refs[18:21]
    own_sems, other_sems, table_sems, phase_sems, out_sems = refs[21:]
    offset = HALF_TILES * core[0]

    def tile_rows(tile):
        if isinstance(tile, int):
            return slice(tile * TILE, (tile + 1) * TILE)
        return pl.ds(pl.multiple_of(tile * TILE, TILE), TILE)

    def own_copy(i):
        return pltpu.make_async_copy(arrived.at[:, pl.ds(TILE * i, TILE)], own.at[i], own_sems.at[i])

    def other_copy(i):
        if i < HALF_TILES:
            source = arrived.at[:, pl.ds(ROWS + TILE * i, TILE)]
        else:
            source = swapped.at[:, pl.ds(TILE * (i - HALF_TILES), TILE)]
        return pltpu.make_async_copy(source, other.at[(i + offset) % TILES], other_sems.at[i])

    def table_copy(n):
        return pltpu.make_async_copy(tables[n], copies[n], table_sems.at[n])

    def phase_copy(q):
        return pltpu.make_async_copy(tables[0].at[q], phases.at[q], phase_sems.at[q])

    def out_copy(i):
        return pltpu.make_async_copy(results.at[i], out.at[:, tile_rows(i)], out_sems.at[i])

    for i in range(TILES):
        own_copy(i).start()
        other_copy(i).start()
    for n in range(1, len(tables)):
        table_copy(n).start()
    for q in range(3):
        phase_copy(q).start()
    for ref in (held_entered, held_multiplied, held_turned, even_back, odd_back):
        ref[...] = jnp.zeros(ref.shape, ref.dtype)

    def over_high(source, slot, number):
        for b in range(8):
            column = []
            for a in range(8):
                c, s = unit(-a / 32.0)
                x = source[slot, slot_of(8 * a + b)]
                column.append((x * c, x * s))
            for q, value in enumerate(dft8(column, -1)):
                r, i = turn(value, -b * (q + 0.25) / 64.0)
                spread[number, slot, 8 * b + q, :, :LANES] = r
                spread[number, slot, 8 * b + q, :, LANES:] = i

    def spread_step(i, carry):
        slot = (i + offset) % TILES
        pltpu.make_async_copy(arrived.at[:, pl.ds(0, TILE)], own.at[i], own_sems.at[i]).wait()
        over_high(own, i, 0)
        pltpu.make_async_copy(arrived.at[:, pl.ds(0, TILE)], other.at[slot], other_sems.at[i]).wait()
        over_high(other, slot, 1)
        return carry

    lax.fori_loop(0, TILES, spread_step, 0)
    for n in range(1, len(tables)):
        table_copy(n).wait()
    for q in range(3, 8):
        phase_copy(q).start()
    phase_copy(0).wait()

    def over_low(q, tile, number, target):
        rows = tile_rows(tile)
        column = []
        for b in range(8):
            at = 8 * b + q
            column.append((spread[number, tile, at, :, :LANES], spread[number, tile, at, :, LANES:]))
        for p, (r, i) in enumerate(dft8(column, -1)):
            c, s = phases[q, p, rows, :LANES], phases[q, p, rows, LANES:]
            target[p, number, rows, :LANES] = r * c + i * s
            target[p, number, rows, LANES:] = i * c - r * s

    def back_low(q, tile, source):
        rows = tile_rows(tile)
        column = []
        for p in range(8):
            r, i = source[p, rows, :LANES], source[p, rows, LANES:]
            c, s = phases[q, p, rows, :LANES], phases[q, p, rows, LANES:]
            column.append((r * c - i * s, i * c + r * s))
        for b, (r, i) in enumerate(dft8(column, 1)):
            gathered[tile, 8 * b + q, :, :LANES] = r
            gathered[tile, 8 * b + q, :, LANES:] = i

    c_inner, s_inner = inner[:, :LANES], inner[:, LANES:]

    def entry_columns(source, first_bin):
        columns = []
        for e in range(SIZE):
            for number in range(2):
                x = source[first_bin + e, number]
                columns.append(jnp.concatenate([x[:, :LANES], x[:, LANES:]], axis=0))
        return columns

    def lanes(y, n):
        at = slice(n * LANES, (n + 1) * LANES)
        return y[:ROWS, at], y[ROWS:, at]

    def entry_rows(y):
        rows = []
        for n in range(2 * SIZE):
            r, i = lanes(y, n)
            rows.append(
                jnp.concatenate(
                    [r * c_inner + i * s_inner, i * c_inner - r * s_inner], axis=1
                )
            )
        return jnp.concatenate(rows, axis=0)

    def product_rows(z):
        made = []
        for e in range(SIZE):
            f = z[2 * e * ROWS : (2 * e + 1) * ROWS]
            g = z[(2 * e + 1) * ROWS : (2 * e + 2) * ROWS]
            fr, fi, gr, gi = f[:, :LANES], f[:, LANES:], g[:, :LANES], g[:, LANES:]
            made.append(jnp.concatenate([gi * fr - gr * fi, gr * fr + gi * fi], axis=1))
        return jnp.concatenate(made, axis=0)

    def exit_columns(z):
        columns = []
        for e in range(SIZE):
            i = z[e * ROWS : (e + 1) * ROWS, :LANES]
            r = z[e * ROWS : (e + 1) * ROWS, LANES:]
            columns.append(
                jnp.concatenate(
                    [i * c_inner + r * s_inner, r * c_inner - i * s_inner], axis=0
                )
            )
        return jnp.concatenate(columns, axis=1)

    def leave(target, first_bin, y, start):
        for e in range(SIZE):
            i, r = lanes(y, start + e)
            target[first_bin + e, :, :LANES] = r
            target[first_bin + e, :, LANES:] = i

    def advance(flight, source, first_bin, target, last_bin):
        entered, multiplied, turned = flight
        leave(target, last_bin, times_left(left[...], turned), 0)
        turned = exit_columns(times_right(multiplied, right[...]))
        multiplied = product_rows(times_right(entered, right[...]))
        if source is not None:
            columns = jnp.concatenate(entry_columns(source, first_bin), axis=1)
            entered = entry_rows(times_left(left[...], columns))
        return entered, multiplied, turned

    def left_at(step):
        return -((step - 3) // STEPS), (step - 3) % STEPS * SIZE

    delay = next(ago for ago, at in map(left_at, range(STEPS)) if at + SIZE == 8)

    def half(flight, now, q_next, then, q_last, backs):
        per_step = 2 * TILES // STEPS
        for step in range(STEPS):
            ago, last_bin = left_at(step)
            flight = advance(flight, now, step * SIZE, backs[ago % 2], last_bin)
            for n in range(step * per_step, (step + 1) * per_step):
                if q_next is not None:
                    over_low(q_next, n // 2, n % 2, then)
            if last_bin + SIZE == 8 and q_last is not None:
                for tile in range(TILES):
                    back_low(q_last, tile, backs[ago % 2])
        return flight

    for tile in range(TILES):
        over_low(0, tile, 0, even)
        over_low(0, tile, 1, even)

    backs_of = ((even_back, odd_back), (odd_back, even_back))
    enter_of = ((even, odd), (odd, even))
    flight = held_entered[...], held_multiplied[...], held_turned[...]
    for q in range(2):
        phase_copy(q + 1).wait()
        flight = half(flight, enter_of[q][0], q + 1, enter_of[q][1], None, backs_of[q])
    held_entered[...], held_multiplied[...], held_turned[...] = flight

    def pair_step(t, carry):
        flight = held_entered[...], held_multiplied[...], held_turned[...]
        for n in range(2):
            phase_copy(2 * t + n + 1).wait()
        for n in range(2):
            q = 2 * t + n
            flight = half(flight, enter_of[n][0], q + 1, enter_of[n][1], q - delay, backs_of[n])
        held_entered[...], held_multiplied[...], held_turned[...] = flight
        return carry

    lax.fori_loop(1, 3, pair_step, 0, unroll=2)
    phase_copy(7).wait()
    flight = held_entered[...], held_multiplied[...], held_turned[...]
    for q in range(6, 8):
        after = q + 1 if q < 7 else None
        flight = half(flight, enter_of[q % 2][0], after, enter_of[q % 2][1], q - delay, backs_of[q % 2])
    for step in range(3):
        ago, last_bin = left_at(step)
        q = 8 - ago
        target = (even_back, odd_back)[q % 2]
        flight = advance(flight, None, 0, target, last_bin)
        if last_bin + SIZE == 8:
            for tile in range(TILES):
                back_low(q, tile, target)

    def gather_step(tile, carry):
        scale = 1.0 / LENGTH
        for b in range(8):
            column = []
            for q in range(8):
                at = 8 * b + q
                value = (gathered[tile, at, :, :LANES], gathered[tile, at, :, LANES:])
                column.append(turn(value, b * (q + 0.25) / 64.0))
            for a, (r, i) in enumerate(dft8(column, 1)):
                c, s = unit(a / 32.0)
                results[tile, slot_of(8 * a + b)] = r * (c * scale) - i * (s * scale)
        out_copy(tile).start()
        return carry

    lax.fori_loop(0, TILES, gather_step, 0)
    for i in range(TILES):
        out_copy(i).wait()


def side_by_side(turns):
    angle = 2.0 * np.pi * turns
    return np.concatenate([np.cos(angle), np.sin(angle)], axis=-1).astype(np.float32)


def outer_phases():
    position = np.arange(ROWS * LANES).reshape(1, ROWS, LANES)
    bins = np.arange(BLOCKS).reshape(8, 8).T.reshape(BLOCKS, 1, 1)
    turns = side_by_side(position * (bins + 0.25) / LENGTH)
    return turns.reshape(8, 8, ROWS, 2 * LANES)


def inner_phases():
    return side_by_side(np.outer(np.arange(ROWS), np.arange(LANES)) / (ROWS * LANES))


def halves(whole):
    high = whole.astype(np.float32).astype(ml_dtypes.bfloat16)
    low = (whole - high.astype(np.float64)).astype(np.float32).astype(ml_dtypes.bfloat16)
    return high, low


def rotation(size):
    angle = 2.0 * np.pi * (np.outer(np.arange(size), np.arange(size)) % size) / size
    c, s = np.cos(angle), np.sin(angle)
    return np.block([[c, s], [-s, c]])


def left_table():
    high, low = halves(rotation(ROWS))
    return np.block([[high, high], [low, np.zeros_like(low)]])


def right_table():
    high, low = halves(rotation(LANES).T)
    return np.concatenate([high, high, low], axis=0)


PARAMS = pltpu.CompilerParams(vmem_limit_bytes=56 * 1024 * 1024)


ANY = pl.BlockSpec(memory_space=pl.ANY)


def pack(signal, cotangent, long_filter, chips):
    groups = signal.shape[0] // TILE
    height = ROWS + ROWS // 2
    return pl.pallas_call(
        pack_kernel,
        in_specs=[ANY] * 3,
        out_specs=ANY,
        out_shape=jax.ShapeDtypeStruct((2, chips, height, LANES), jnp.float32),
        scratch_shapes=[
            pltpu.VMEM((groups, 3, TILE, ROWS * LANES), jnp.float32),
            pltpu.VMEM((groups, 2, TILE, height, LANES), jnp.float32),
            pltpu.SemaphoreType.DMA((groups, 3)),
            pltpu.SemaphoreType.DMA((chips // TILE, 3)),
        ],
        compiler_params=PARAMS,
        name="pack",
    )(signal, cotangent, long_filter)


def unpack(landed, channels):
    groups = channels // TILE
    result = jax.ShapeDtypeStruct((channels, ROWS * LANES), jnp.float32)
    return pl.pallas_call(
        unpack_kernel,
        in_specs=[ANY],
        out_specs=[ANY, ANY],
        out_shape=[result, result],
        scratch_shapes=[
            pltpu.VMEM((groups, 2, TILE, ROWS, LANES), jnp.float32),
            pltpu.VMEM((groups, 2, TILE, ROWS * LANES), jnp.float32),
            pltpu.SemaphoreType.DMA((groups, 2)),
            pltpu.SemaphoreType.DMA((groups, 2)),
        ],
        compiler_params=PARAMS,
        name="unpack",
    )(landed)


def correlate(core, arrived, swapped):
    tables = [
        outer_phases(),
        left_table(),
        inner_phases(),
        right_table(),
    ]
    tile = (TILES, BLOCKS, TILE, LANES)
    return pl.pallas_call(
        correlate_kernel,
        in_specs=[pl.BlockSpec(memory_space=pltpu.SMEM)] + [ANY] * (2 + len(tables)),
        out_specs=ANY,
        out_shape=jax.ShapeDtypeStruct((BLOCKS, ROWS, LANES), jnp.float32),
        scratch_shapes=[pltpu.VMEM(table.shape, table.dtype) for table in tables]
        + [
            pltpu.VMEM(tile, jnp.float32),
            pltpu.VMEM(tile, jnp.float32),
            pltpu.VMEM((2, TILES, BLOCKS, TILE, 2 * LANES), jnp.float32),
            pltpu.VMEM((8, 2, ROWS, 2 * LANES), jnp.float32),
            pltpu.VMEM((8, 2, ROWS, 2 * LANES), jnp.float32),
            pltpu.VMEM((8, ROWS, 2 * LANES), jnp.float32),
            pltpu.VMEM((8, ROWS, 2 * LANES), jnp.float32),
            pltpu.VMEM((TILES, BLOCKS, TILE, 2 * LANES), jnp.float32),
            pltpu.VMEM(tile, jnp.float32),
            pltpu.VMEM((2 * SIZE * ROWS, 2 * LANES), jnp.float32),
            pltpu.VMEM((SIZE * ROWS, 2 * LANES), jnp.float32),
            pltpu.VMEM((2 * ROWS, SIZE * LANES), jnp.float32),
            pltpu.SemaphoreType.DMA((TILES,)),
            pltpu.SemaphoreType.DMA((TILES,)),
            pltpu.SemaphoreType.DMA((len(tables),)),
            pltpu.SemaphoreType.DMA((8,)),
            pltpu.SemaphoreType.DMA((TILES,)),
        ],
        compiler_params=PARAMS,
        name="correlate",
    )(core, arrived, swapped, *tables)


def exchange(blocks):
    return lax.all_to_all(blocks, LISTED, split_axis=0, concat_axis=0, tiled=True)


def on_device(signal, cotangent, long_filter):
    channels = signal.shape[0]
    packed = pack(signal, cotangent, long_filter, BLOCKS // 2)
    arrived = exchange(packed.reshape(BLOCKS, *packed.shape[2:]))
    swapped = lax.ppermute(arrived[:, ROWS:], "core", [(0, 1), (1, 0)])
    core = lax.axis_index("core").astype(jnp.int32).reshape(1)
    landed = exchange(correlate(core, arrived, swapped))
    return tuple(unpack(landed.reshape(2, BLOCKS // 2, ROWS, LANES), channels))


def solution(mesh):
    digits = Mesh(mesh.devices.reshape(4, 4, 2, 2, 2), SEQUENCE + ("chan",))
    spec = P("chan", SEQUENCE)
    return jax.shard_map(
        on_device, mesh=digits, in_specs=(spec,) * 3, out_specs=(spec,) * 2, check_vma=False
    )
```

```python
import math

import jax
import jax.numpy as jnp
import ml_dtypes
import numpy as np
from jax import lax
from jax.experimental import pallas as pl
from jax.experimental.pallas import tpu as pltpu
from jax.sharding import Mesh, PartitionSpec as P

LANES = 128
BLOCKS = 64
ROWS = 64
TILE = 8
TILES = ROWS // TILE
HALF_TILES = TILES // 2
SIZE = 4
STEPS = 8 // SIZE
LENGTH = BLOCKS * ROWS * LANES
SEQUENCE = ("z", "y", "xh", "core")
LISTED = ("core", "z", "xh", "y")
ROOT_HALF = math.sqrt(0.5)


def slot_of(block):
    z, y, xh, core = block // 16, block // 4 % 4, block // 2 % 2, block % 2
    return 32 * core + 8 * z + 4 * xh + y


def unit(turns):
    return (math.cos(2.0 * math.pi * turns), math.sin(2.0 * math.pi * turns))


def plus(a, b):
    return (a[0] + b[0], a[1] + b[1])


def minus(a, b):
    return (a[0] - b[0], a[1] - b[1])


def turn(a, turns):
    turns = turns % 1.0
    if turns == 0.0:
        return a
    c, s = unit(turns)
    return (a[0] * c - a[1] * s, a[1] * c + a[0] * s)


def quarter(a, sign):
    if sign > 0:
        return (-a[1], a[0])
    return (a[1], -a[0])


def dft4(v, sign):
    t0, t1 = plus(v[0], v[2]), minus(v[0], v[2])
    t2, t3 = plus(v[1], v[3]), quarter(minus(v[1], v[3]), sign)
    return [plus(t0, t2), plus(t1, t3), minus(t0, t2), minus(t1, t3)]


def dft8(v, sign):
    up = [plus(v[n], v[n + 4]) for n in range(4)]
    down = [minus(v[n], v[n + 4]) for n in range(4)]
    r, i = down[1]
    down[1] = ((r - sign * i) * ROOT_HALF, (i + sign * r) * ROOT_HALF)
    down[2] = quarter(down[2], sign)
    r, i = down[3]
    down[3] = ((-r - sign * i) * ROOT_HALF, (sign * r - i) * ROOT_HALF)
    even, odd = dft4(up, sign), dft4(down, sign)
    return [even[k // 2] if k % 2 == 0 else odd[k // 2] for k in range(8)]


def split(rows):
    high = rows.astype(jnp.bfloat16)
    return high, (rows - high.astype(jnp.float32)).astype(jnp.bfloat16)


def times_right(rows, table):
    high, low = split(rows)
    return jnp.dot(
        jnp.concatenate([high, low, high], axis=1), table, preferred_element_type=jnp.float32
    )


def times_left(table, columns):
    high, low = split(columns)
    both = jnp.dot(
        table, jnp.concatenate([high, low], axis=0), preferred_element_type=jnp.float32
    )
    return both[: 2 * ROWS] + both[2 * ROWS :]


def pack_kernel(signal, cotangent, long_filter, out, taken, packed, in_sems, out_sems):
    groups = signal.shape[0] // TILE
    slots = out.shape[1] // TILE
    sources = (long_filter, signal, cotangent)

    def arrival(g, n):
        rows = pl.ds(TILE * g, TILE)
        return pltpu.make_async_copy(sources[n].at[rows], taken.at[g, n], in_sems.at[g, n])

    def departure(slot, n):
        g = min(slot, groups - 1)
        chips = pl.ds(TILE * slot, TILE)
        if n < 2:
            rows = pl.ds(0, ROWS)
            source, target = packed.at[g, n, :, rows], out.at[n, chips, rows]
        else:
            rows = pl.ds(ROWS, ROWS // 2)
            source, target = packed.at[g, :, :, rows], out.at[:, chips, rows]
        return pltpu.make_async_copy(source, target, out_sems.at[slot, n])

    for g in range(groups):
        for n in range(3):
            arrival(g, n).start()
    for g in range(groups):
        for n in range(3):
            arrival(g, n).wait()
            for u in range(TILES):
                slabs = [
                    taken[g, n, :, (TILE * u + v) * LANES : (TILE * u + v + 1) * LANES]
                    for v in range(TILE)
                ]
                turned = jnp.swapaxes(jnp.stack(slabs), 0, 1)
                if n < 2:
                    packed[g, n, :, TILE * u : TILE * (u + 1)] = turned
                else:
                    low = ROWS + TILE * (u % HALF_TILES)
                    packed[g, u // HALF_TILES, :, low : low + TILE] = turned
            departure(g, n).start()
    for slot in range(groups, slots):
        for n in range(3):
            departure(slot, n).start()
    for slot in range(slots):
        for n in range(3):
            departure(slot, n).wait()


def unpack_kernel(landed, grad_signal, grad_filter, taken, turned_out, in_sems, out_sems):
    groups = grad_signal.shape[0] // TILE
    targets = (grad_signal, grad_filter)

    def arrival(g, n):
        chips = pl.ds(TILE * g, TILE)
        return pltpu.make_async_copy(landed.at[n, chips], taken.at[g, n], in_sems.at[g, n])

    def departure(g, n):
        rows = pl.ds(TILE * g, TILE)
        return pltpu.make_async_copy(turned_out.at[g, n], targets[n].at[rows], out_sems.at[g, n])

    for g in range(groups):
        for n in range(2):
            arrival(g, n).start()
    for g in range(groups):
        for n in range(2):
            arrival(g, n).wait()
            for u in range(TILES):
                turned = jnp.swapaxes(taken[g, n, :, TILE * u : TILE * (u + 1)], 0, 1)
                for v in range(TILE):
                    at = (TILE * u + v) * LANES
                    turned_out[g, n, :, at : at + LANES] = turned[v]
            departure(g, n).start()
    for g in range(groups):
        for n in range(2):
            departure(g, n).wait()


def correlate_kernel(core, arrived, swapped, *refs):
    tables, out, copies = refs[:4], refs[4], refs[5:9]
    phases, left, inner, right = copies
    own, other, spread, even, odd, even_back, odd_back, gathered, results = refs[9:18]
    held_entered, held_multiplied, held_turned = refs[18:21]
    own_sems, other_sems, table_sems, phase_sems, out_sems = refs[21:]
    offset = HALF_TILES * core[0]

    def tile_rows(tile):
        if isinstance(tile, int):
            return slice(tile * TILE, (tile + 1) * TILE)
        return pl.ds(pl.multiple_of(tile * TILE, TILE), TILE)

    def own_copy(i):
        return pltpu.make_async_copy(arrived.at[:, pl.ds(TILE * i, TILE)], own.at[i], own_sems.at[i])

    def other_copy(i):
        if i < HALF_TILES:
            source = arrived.at[:, pl.ds(ROWS + TILE * i, TILE)]
        else:
            source = swapped.at[:, pl.ds(TILE * (i - HALF_TILES), TILE)]
        return pltpu.make_async_copy(source, other.at[(i + offset) % TILES], other_sems.at[i])

    def table_copy(n):
        return pltpu.make_async_copy(tables[n], copies[n], table_sems.at[n])

    def phase_copy(q):
        return pltpu.make_async_copy(tables[0].at[q], phases.at[q], phase_sems.at[q])

    def out_copy(i):
        return pltpu.make_async_copy(results.at[i], out.at[:, tile_rows(i)], out_sems.at[i])

    for i in range(TILES):
        own_copy(i).start()
        other_copy(i).start()
    for n in range(1, len(tables)):
        table_copy(n).start()
    for q in range(3):
        phase_copy(q).start()
    for ref in (held_entered, held_multiplied, held_turned, even_back, odd_back):
        ref[...] = jnp.zeros(ref.shape, ref.dtype)

    def over_high(source, slot, number):
        for b in range(8):
            column = []
            for a in range(8):
                c, s = unit(-a / 32.0)
                x = source[slot, slot_of(8 * a + b)]
                column.append((x * c, x * s))
            for q, value in enumerate(dft8(column, -1)):
                r, i = turn(value, -b * (q + 0.25) / 64.0)
                spread[number, slot, 8 * b + q, :, :LANES] = r
                spread[number, slot, 8 * b + q, :, LANES:] = i

    def spread_step(i, carry):
        slot = (i + offset) % TILES
        pltpu.make_async_copy(arrived.at[:, pl.ds(0, TILE)], own.at[i], own_sems.at[i]).wait()
        over_high(own, i, 0)
        pltpu.make_async_copy(arrived.at[:, pl.ds(0, TILE)], other.at[slot], other_sems.at[i]).wait()
        over_high(other, slot, 1)
        return carry

    lax.fori_loop(0, TILES, spread_step, 0)
    for n in range(1, len(tables)):
        table_copy(n).wait()
    for q in range(3, 8):
        phase_copy(q).start()
    phase_copy(0).wait()

    def over_low(q, tile, number, target):
        rows = tile_rows(tile)
        column = []
        for b in range(8):
            at = 8 * b + q
            column.append((spread[number, tile, at, :, :LANES], spread[number, tile, at, :, LANES:]))
        for p, (r, i) in enumerate(dft8(column, -1)):
            c, s = phases[q, p, rows, :LANES], phases[q, p, rows, LANES:]
            target[p, number, rows, :LANES] = r * c + i * s
            target[p, number, rows, LANES:] = i * c - r * s

    def back_low(q, tile, source):
        rows = tile_rows(tile)
        column = []
        for p in range(8):
            r, i = source[p, rows, :LANES], source[p, rows, LANES:]
            c, s = phases[q, p, rows, :LANES], phases[q, p, rows, LANES:]
            column.append((r * c - i * s, i * c + r * s))
        for b, (r, i) in enumerate(dft8(column, 1)):
            gathered[tile, 8 * b + q, :, :LANES] = r
            gathered[tile, 8 * b + q, :, LANES:] = i

    c_inner, s_inner = inner[:, :LANES], inner[:, LANES:]

    def entry_columns(source, first_bin):
        columns = []
        for e in range(SIZE):
            for number in range(2):
                x = source[first_bin + e, number]
                columns.append(jnp.concatenate([x[:, :LANES], x[:, LANES:]], axis=0))
        return columns

    def lanes(y, n):
        at = slice(n * LANES, (n + 1) * LANES)
        return y[:ROWS, at], y[ROWS:, at]

    def entry_rows(y):
        rows = []
        for n in range(2 * SIZE):
            r, i = lanes(y, n)
            rows.append(
                jnp.concatenate(
                    [r * c_inner + i * s_inner, i * c_inner - r * s_inner], axis=1
                )
            )
        return jnp.concatenate(rows, axis=0)

    def product_rows(z):
        made = []
        for e in range(SIZE):
            f = z[2 * e * ROWS : (2 * e + 1) * ROWS]
            g = z[(2 * e + 1) * ROWS : (2 * e + 2) * ROWS]
            fr, fi, gr, gi = f[:, :LANES], f[:, LANES:], g[:, :LANES], g[:, LANES:]
            made.append(jnp.concatenate([gi * fr - gr * fi, gr * fr + gi * fi], axis=1))
        return jnp.concatenate(made, axis=0)

    def exit_columns(z):
        columns = []
        for e in range(SIZE):
            i = z[e * ROWS : (e + 1) * ROWS, :LANES]
            r = z[e * ROWS : (e + 1) * ROWS, LANES:]
            columns.append(
                jnp.concatenate(
                    [i * c_inner + r * s_inner, r * c_inner - i * s_inner], axis=0
                )
            )
        return jnp.concatenate(columns, axis=1)

    def leave(target, first_bin, y, start):
        for e in range(SIZE):
            i, r = lanes(y, start + e)
            target[first_bin + e, :, :LANES] = r
            target[first_bin + e, :, LANES:] = i

    def advance(flight, source, first_bin, target, last_bin):
        entered, multiplied, turned = flight
        leave(target, last_bin, times_left(left[...], turned), 0)
        turned = exit_columns(times_right(multiplied, right[...]))
        multiplied = product_rows(times_right(entered, right[...]))
        if source is not None:
            columns = jnp.concatenate(entry_columns(source, first_bin), axis=1)
            entered = entry_rows(times_left(left[...], columns))
        return entered, multiplied, turned

    def left_at(step):
        return -((step - 3) // STEPS), (step - 3) % STEPS * SIZE

    delay = next(ago for ago, at in map(left_at, range(STEPS)) if at + SIZE == 8)

    def half(flight, now, q_next, then, q_last, backs):
        per_step = 2 * TILES // STEPS
        for step in range(STEPS):
            ago, last_bin = left_at(step)
            flight = advance(flight, now, step * SIZE, backs[ago % 2], last_bin)
            for n in range(step * per_step, (step + 1) * per_step):
                if q_next is not None:
                    over_low(q_next, n // 2, n % 2, then)
            if last_bin + SIZE == 8 and q_last is not None:
                for tile in range(TILES):
                    back_low(q_last, tile, backs[ago % 2])
        return flight

    for tile in range(TILES):
        over_low(0, tile, 0, even)
        over_low(0, tile, 1, even)

    backs_of = ((even_back, odd_back), (odd_back, even_back))
    enter_of = ((even, odd), (odd, even))
    flight = held_entered[...], held_multiplied[...], held_turned[...]
    for q in range(2):
        phase_copy(q + 1).wait()
        flight = half(flight, enter_of[q][0], q + 1, enter_of[q][1], None, backs_of[q])
    held_entered[...], held_multiplied[...], held_turned[...] = flight

    def pair_step(t, carry):
        flight = held_entered[...], held_multiplied[...], held_turned[...]
        for n in range(2):
            phase_copy(2 * t + n + 1).wait()
        for n in range(2):
            q = 2 * t + n
            flight = half(flight, enter_of[n][0], q + 1, enter_of[n][1], q - delay, backs_of[n])
        held_entered[...], held_multiplied[...], held_turned[...] = flight
        return carry

    lax.fori_loop(1, 3, pair_step, 0, unroll=2)
    phase_copy(7).wait()
    flight = held_entered[...], held_multiplied[...], held_turned[...]
    for q in range(6, 8):
        after = q + 1 if q < 7 else None
        flight = half(flight, enter_of[q % 2][0], after, enter_of[q % 2][1], q - delay, backs_of[q % 2])
    for step in range(3):
        ago, last_bin = left_at(step)
        q = 8 - ago
        target = (even_back, odd_back)[q % 2]
        flight = advance(flight, None, 0, target, last_bin)
        if last_bin + SIZE == 8:
            for tile in range(TILES):
                back_low(q, tile, target)

    def gather_step(tile, carry):
        scale = 1.0 / LENGTH
        for b in range(8):
            column = []
            for q in range(8):
                at = 8 * b + q
                value = (gathered[tile, at, :, :LANES], gathered[tile, at, :, LANES:])
                column.append(turn(value, b * (q + 0.25) / 64.0))
            for a, (r, i) in enumerate(dft8(column, 1)):
                c, s = unit(a / 32.0)
                results[tile, slot_of(8 * a + b)] = r * (c * scale) - i * (s * scale)
        out_copy(tile).start()
        return carry

    lax.fori_loop(0, TILES, gather_step, 0)
    for i in range(TILES):
        out_copy(i).wait()


def side_by_side(turns):
    angle = 2.0 * np.pi * turns
    return np.concatenate([np.cos(angle), np.sin(angle)], axis=-1).astype(np.float32)


def outer_phases():
    position = np.arange(ROWS * LANES).reshape(1, ROWS, LANES)
    bins = np.arange(BLOCKS).reshape(8, 8).T.reshape(BLOCKS, 1, 1)
    turns = side_by_side(position * (bins + 0.25) / LENGTH)
    return turns.reshape(8, 8, ROWS, 2 * LANES)


def inner_phases():
    return side_by_side(np.outer(np.arange(ROWS), np.arange(LANES)) / (ROWS * LANES))


def halves(whole):
    high = whole.astype(np.float32).astype(ml_dtypes.bfloat16)
    low = (whole - high.astype(np.float64)).astype(np.float32).astype(ml_dtypes.bfloat16)
    return high, low


def rotation(size):
    angle = 2.0 * np.pi * (np.outer(np.arange(size), np.arange(size)) % size) / size
    c, s = np.cos(angle), np.sin(angle)
    return np.block([[c, s], [-s, c]])


def left_table():
    high, low = halves(rotation(ROWS))
    return np.block([[high, high], [low, np.zeros_like(low)]])


def right_table():
    high, low = halves(rotation(LANES).T)
    return np.concatenate([high, high, low], axis=0)


MIB = 1024 * 1024
PARAMS = pltpu.CompilerParams(vmem_limit_bytes=56 * MIB)


ANY = pl.BlockSpec(memory_space=pl.ANY)


def pack(signal, cotangent, long_filter, chips):
    groups = signal.shape[0] // TILE
    height = ROWS + ROWS // 2
    return pl.pallas_call(
        pack_kernel,
        in_specs=[ANY] * 3,
        out_specs=ANY,
        out_shape=jax.ShapeDtypeStruct((2, chips, height, LANES), jnp.float32),
        scratch_shapes=[
            pltpu.VMEM((groups, 3, TILE, ROWS * LANES), jnp.float32),
            pltpu.VMEM((groups, 2, TILE, height, LANES), jnp.float32),
            pltpu.SemaphoreType.DMA((groups, 3)),
            pltpu.SemaphoreType.DMA((chips // TILE, 3)),
        ],
        compiler_params=PARAMS,
        name="pack",
    )(signal, cotangent, long_filter)


def unpack(landed, channels):
    groups = channels // TILE
    result = jax.ShapeDtypeStruct((channels, ROWS * LANES), jnp.float32)
    return pl.pallas_call(
        unpack_kernel,
        in_specs=[ANY],
        out_specs=[ANY, ANY],
        out_shape=[result, result],
        scratch_shapes=[
            pltpu.VMEM((groups, 2, TILE, ROWS, LANES), jnp.float32),
            pltpu.VMEM((groups, 2, TILE, ROWS * LANES), jnp.float32),
            pltpu.SemaphoreType.DMA((groups, 2)),
            pltpu.SemaphoreType.DMA((groups, 2)),
        ],
        compiler_params=pltpu.CompilerParams(vmem_limit_bytes=16 * MIB),
        name="unpack",
    )(landed)


def correlate(core, arrived, swapped):
    tables = [
        outer_phases(),
        left_table(),
        inner_phases(),
        right_table(),
    ]
    tile = (TILES, BLOCKS, TILE, LANES)
    return pl.pallas_call(
        correlate_kernel,
        in_specs=[pl.BlockSpec(memory_space=pltpu.SMEM)] + [ANY] * (2 + len(tables)),
        out_specs=ANY,
        out_shape=jax.ShapeDtypeStruct((BLOCKS, ROWS, LANES), jnp.float32),
        scratch_shapes=[pltpu.VMEM(table.shape, table.dtype) for table in tables]
        + [
            pltpu.VMEM(tile, jnp.float32),
            pltpu.VMEM(tile, jnp.float32),
            pltpu.VMEM((2, TILES, BLOCKS, TILE, 2 * LANES), jnp.float32),
            pltpu.VMEM((8, 2, ROWS, 2 * LANES), jnp.float32),
            pltpu.VMEM((8, 2, ROWS, 2 * LANES), jnp.float32),
            pltpu.VMEM((8, ROWS, 2 * LANES), jnp.float32),
            pltpu.VMEM((8, ROWS, 2 * LANES), jnp.float32),
            pltpu.VMEM((TILES, BLOCKS, TILE, 2 * LANES), jnp.float32),
            pltpu.VMEM(tile, jnp.float32),
            pltpu.VMEM((2 * SIZE * ROWS, 2 * LANES), jnp.float32),
            pltpu.VMEM((SIZE * ROWS, 2 * LANES), jnp.float32),
            pltpu.VMEM((2 * ROWS, SIZE * LANES), jnp.float32),
            pltpu.SemaphoreType.DMA((TILES,)),
            pltpu.SemaphoreType.DMA((TILES,)),
            pltpu.SemaphoreType.DMA((len(tables),)),
            pltpu.SemaphoreType.DMA((8,)),
            pltpu.SemaphoreType.DMA((TILES,)),
        ],
        compiler_params=pltpu.CompilerParams(vmem_limit_bytes=40 * MIB),
        name="correlate",
    )(core, arrived, swapped, *tables)


def exchange(blocks):
    return lax.all_to_all(blocks, LISTED, split_axis=0, concat_axis=0, tiled=True)


def on_device(signal, cotangent, long_filter):
    channels = signal.shape[0]
    packed = pack(signal, cotangent, long_filter, BLOCKS // 2)
    arrived = exchange(packed.reshape(BLOCKS, *packed.shape[2:]))
    swapped = lax.ppermute(arrived[:, ROWS:], "core", [(0, 1), (1, 0)])
    core = lax.axis_index("core").astype(jnp.int32).reshape(1)
    landed = exchange(correlate(core, arrived, swapped))
    return tuple(unpack(landed.reshape(2, BLOCKS // 2, ROWS, LANES), channels))


def solution(mesh):
    digits = Mesh(mesh.devices.reshape(4, 4, 2, 2, 2), SEQUENCE + ("chan",))
    spec = P("chan", SEQUENCE)
    return jax.shard_map(
        on_device, mesh=digits, in_specs=(spec,) * 3, out_specs=(spec,) * 2, check_vma=False
    )
```

```python
import math

import jax
import jax.numpy as jnp
import ml_dtypes
import numpy as np
from jax import lax
from jax.experimental import pallas as pl
from jax.experimental.pallas import tpu as pltpu
from jax.sharding import Mesh, PartitionSpec as P

LANES = 128
BLOCKS = 64
ROWS = 64
TILE = 8
TILES = ROWS // TILE
HALF_TILES = TILES // 2
SIZE = 4
STEPS = 8 // SIZE
LENGTH = BLOCKS * ROWS * LANES
SEQUENCE = ("z", "y", "xh", "core")
LISTED = ("core", "z", "xh", "y")
ROOT_HALF = math.sqrt(0.5)


def slot_of(block):
    z, y, xh, core = block // 16, block // 4 % 4, block // 2 % 2, block % 2
    return 32 * core + 8 * z + 4 * xh + y


def unit(turns):
    return (math.cos(2.0 * math.pi * turns), math.sin(2.0 * math.pi * turns))


def plus(a, b):
    return (a[0] + b[0], a[1] + b[1])


def minus(a, b):
    return (a[0] - b[0], a[1] - b[1])


def turn(a, turns):
    turns = turns % 1.0
    if turns == 0.0:
        return a
    c, s = unit(turns)
    return (a[0] * c - a[1] * s, a[1] * c + a[0] * s)


def quarter(a, sign):
    if sign > 0:
        return (-a[1], a[0])
    return (a[1], -a[0])


def dft4(v, sign):
    t0, t1 = plus(v[0], v[2]), minus(v[0], v[2])
    t2, t3 = plus(v[1], v[3]), quarter(minus(v[1], v[3]), sign)
    return [plus(t0, t2), plus(t1, t3), minus(t0, t2), minus(t1, t3)]


def dft8(v, sign):
    up = [plus(v[n], v[n + 4]) for n in range(4)]
    down = [minus(v[n], v[n + 4]) for n in range(4)]
    r, i = down[1]
    down[1] = ((r - sign * i) * ROOT_HALF, (i + sign * r) * ROOT_HALF)
    down[2] = quarter(down[2], sign)
    r, i = down[3]
    down[3] = ((-r - sign * i) * ROOT_HALF, (sign * r - i) * ROOT_HALF)
    even, odd = dft4(up, sign), dft4(down, sign)
    return [even[k // 2] if k % 2 == 0 else odd[k // 2] for k in range(8)]


def split(rows):
    high = rows.astype(jnp.bfloat16)
    return high, (rows - high.astype(jnp.float32)).astype(jnp.bfloat16)


def times_right(rows, table):
    high, low = split(rows)
    return jnp.dot(
        jnp.concatenate([high, low, high], axis=1), table, preferred_element_type=jnp.float32
    )


def times_left(table, columns):
    high, low = split(columns)
    both = jnp.dot(
        table, jnp.concatenate([high, low], axis=0), preferred_element_type=jnp.float32
    )
    return both[: 2 * ROWS] + both[2 * ROWS :]


def pack_kernel(signal, cotangent, long_filter, out, taken, packed, in_sems, out_sems):
    groups = signal.shape[0] // TILE
    slots = out.shape[1] // TILE
    sources = (long_filter, signal, cotangent)

    def arrival(g, n):
        rows = pl.ds(TILE * g, TILE)
        return pltpu.make_async_copy(sources[n].at[rows], taken.at[g, n], in_sems.at[g, n])

    def departure(slot, n):
        g = min(slot, groups - 1)
        chips = pl.ds(TILE * slot, TILE)
        if n < 2:
            rows = pl.ds(0, ROWS)
            source, target = packed.at[g, n, :, rows], out.at[n, chips, rows]
        else:
            rows = pl.ds(ROWS, ROWS // 2)
            source, target = packed.at[g, :, :, rows], out.at[:, chips, rows]
        return pltpu.make_async_copy(source, target, out_sems.at[slot, n])

    for g in range(groups):
        for n in range(3):
            arrival(g, n).start()
    for g in range(groups):
        for n in range(3):
            arrival(g, n).wait()
            for u in range(TILES):
                slabs = [
                    taken[g, n, :, (TILE * u + v) * LANES : (TILE * u + v + 1) * LANES]
                    for v in range(TILE)
                ]
                turned = jnp.swapaxes(jnp.stack(slabs), 0, 1)
                if n < 2:
                    packed[g, n, :, TILE * u : TILE * (u + 1)] = turned
                else:
                    low = ROWS + TILE * (u % HALF_TILES)
                    packed[g, u // HALF_TILES, :, low : low + TILE] = turned
            departure(g, n).start()
    for slot in range(groups, slots):
        for n in range(3):
            departure(slot, n).start()
    for slot in range(slots):
        for n in range(3):
            departure(slot, n).wait()


def unpack_kernel(landed, grad_signal, grad_filter, taken, turned_out, in_sems, out_sems):
    groups = grad_signal.shape[0] // TILE
    targets = (grad_signal, grad_filter)

    def arrival(g, n):
        chips = pl.ds(TILE * g, TILE)
        return pltpu.make_async_copy(landed.at[n, chips], taken.at[g, n], in_sems.at[g, n])

    def departure(g, n):
        rows = pl.ds(TILE * g, TILE)
        return pltpu.make_async_copy(turned_out.at[g, n], targets[n].at[rows], out_sems.at[g, n])

    for g in range(groups):
        for n in range(2):
            arrival(g, n).start()
    for g in range(groups):
        for n in range(2):
            arrival(g, n).wait()
            for u in range(TILES):
                turned = jnp.swapaxes(taken[g, n, :, TILE * u : TILE * (u + 1)], 0, 1)
                for v in range(TILE):
                    at = (TILE * u + v) * LANES
                    turned_out[g, n, :, at : at + LANES] = turned[v]
            departure(g, n).start()
    for g in range(groups):
        for n in range(2):
            departure(g, n).wait()


def correlate_kernel(core, arrived, swapped, *refs):
    tables, out, copies = refs[:4], refs[4], refs[5:9]
    phases, left, inner, right = copies
    own, other, spread, even, odd, even_back, odd_back, gathered, results = refs[9:18]
    held_entered, held_multiplied, held_turned = refs[18:21]
    own_sems, other_sems, table_sems, phase_sems, out_sems = refs[21:]
    offset = HALF_TILES * core[0]

    def tile_rows(tile):
        if isinstance(tile, int):
            return slice(tile * TILE, (tile + 1) * TILE)
        return pl.ds(pl.multiple_of(tile * TILE, TILE), TILE)

    def own_copy(i):
        return pltpu.make_async_copy(arrived.at[:, pl.ds(TILE * i, TILE)], own.at[i], own_sems.at[i])

    def other_copy(i):
        if i < HALF_TILES:
            source = arrived.at[:, pl.ds(ROWS + TILE * i, TILE)]
        else:
            source = swapped.at[:, pl.ds(TILE * (i - HALF_TILES), TILE)]
        return pltpu.make_async_copy(source, other.at[(i + offset) % TILES], other_sems.at[i])

    def table_copy(n):
        return pltpu.make_async_copy(tables[n], copies[n], table_sems.at[n])

    def phase_copy(q):
        return pltpu.make_async_copy(tables[0].at[q], phases.at[q], phase_sems.at[q])

    def out_copy(i):
        return pltpu.make_async_copy(results.at[i], out.at[:, tile_rows(i)], out_sems.at[i])

    for i in range(TILES):
        own_copy(i).start()
        other_copy(i).start()
    for n in range(1, len(tables)):
        table_copy(n).start()
    for q in range(3):
        phase_copy(q).start()
    for ref in (held_entered, held_multiplied, held_turned, even_back, odd_back):
        ref[...] = jnp.zeros(ref.shape, ref.dtype)

    def over_high(source, slot, number):
        for b in range(8):
            column = []
            for a in range(8):
                c, s = unit(-a / 32.0)
                x = source[slot, slot_of(8 * a + b)]
                column.append((x * c, x * s))
            for q, value in enumerate(dft8(column, -1)):
                r, i = turn(value, -b * (q + 0.25) / 64.0)
                spread[number, slot, 8 * b + q, :, :LANES] = r
                spread[number, slot, 8 * b + q, :, LANES:] = i

    def spread_step(i, carry):
        slot = (i + offset) % TILES
        pltpu.make_async_copy(arrived.at[:, pl.ds(0, TILE)], own.at[i], own_sems.at[i]).wait()
        over_high(own, i, 0)
        pltpu.make_async_copy(arrived.at[:, pl.ds(0, TILE)], other.at[slot], other_sems.at[i]).wait()
        over_high(other, slot, 1)
        return carry

    lax.fori_loop(0, TILES, spread_step, 0)
    for n in range(1, len(tables)):
        table_copy(n).wait()
    for q in range(3, 8):
        phase_copy(q).start()
    phase_copy(0).wait()

    def over_low(q, tile, number, target):
        rows = tile_rows(tile)
        column = []
        for b in range(8):
            at = 8 * b + q
            column.append((spread[number, tile, at, :, :LANES], spread[number, tile, at, :, LANES:]))
        for p, (r, i) in enumerate(dft8(column, -1)):
            c, s = phases[q, p, rows, :LANES], phases[q, p, rows, LANES:]
            target[p, number, rows, :LANES] = r * c + i * s
            target[p, number, rows, LANES:] = i * c - r * s

    def back_low(q, tile, source):
        rows = tile_rows(tile)
        column = []
        for p in range(8):
            r, i = source[p, rows, :LANES], source[p, rows, LANES:]
            c, s = phases[q, p, rows, :LANES], phases[q, p, rows, LANES:]
            column.append((r * c - i * s, i * c + r * s))
        for b, (r, i) in enumerate(dft8(column, 1)):
            gathered[tile, 8 * b + q, :, :LANES] = r
            gathered[tile, 8 * b + q, :, LANES:] = i

    c_inner, s_inner = inner[:, :LANES], inner[:, LANES:]

    def entry_columns(source, first_bin):
        columns = []
        for e in range(SIZE):
            for number in range(2):
                x = source[first_bin + e, number]
                columns.append(jnp.concatenate([x[:, :LANES], x[:, LANES:]], axis=0))
        return columns

    def lanes(y, n):
        at = slice(n * LANES, (n + 1) * LANES)
        return y[:ROWS, at], y[ROWS:, at]

    def entry_rows(y):
        rows = []
        for n in range(2 * SIZE):
            r, i = lanes(y, n)
            rows.append(
                jnp.concatenate(
                    [r * c_inner + i * s_inner, i * c_inner - r * s_inner], axis=1
                )
            )
        return jnp.concatenate(rows, axis=0)

    def product_rows(z):
        made = []
        for e in range(SIZE):
            f = z[2 * e * ROWS : (2 * e + 1) * ROWS]
            g = z[(2 * e + 1) * ROWS : (2 * e + 2) * ROWS]
            fr, fi, gr, gi = f[:, :LANES], f[:, LANES:], g[:, :LANES], g[:, LANES:]
            made.append(jnp.concatenate([gi * fr - gr * fi, gr * fr + gi * fi], axis=1))
        return jnp.concatenate(made, axis=0)

    def exit_columns(z):
        columns = []
        for e in range(SIZE):
            i = z[e * ROWS : (e + 1) * ROWS, :LANES]
            r = z[e * ROWS : (e + 1) * ROWS, LANES:]
            columns.append(
                jnp.concatenate(
                    [i * c_inner + r * s_inner, r * c_inner - i * s_inner], axis=0
                )
            )
        return jnp.concatenate(columns, axis=1)

    def leave(target, first_bin, y, start):
        for e in range(SIZE):
            i, r = lanes(y, start + e)
            target[first_bin + e, :, :LANES] = r
            target[first_bin + e, :, LANES:] = i

    def advance(flight, source, first_bin, target, last_bin):
        entered, multiplied, turned = flight
        leave(target, last_bin, times_left(left[...], turned), 0)
        turned = exit_columns(times_right(multiplied, right[...]))
        multiplied = product_rows(times_right(entered, right[...]))
        if source is not None:
            columns = jnp.concatenate(entry_columns(source, first_bin), axis=1)
            entered = entry_rows(times_left(left[...], columns))
        return entered, multiplied, turned

    def left_at(step):
        return -((step - 3) // STEPS), (step - 3) % STEPS * SIZE

    delay = next(ago for ago, at in map(left_at, range(STEPS)) if at + SIZE == 8)

    def half(flight, now, q_next, then, q_last, backs):
        per_step = 2 * TILES // STEPS
        for step in range(STEPS):
            ago, last_bin = left_at(step)
            flight = advance(flight, now, step * SIZE, backs[ago % 2], last_bin)
            for n in range(step * per_step, (step + 1) * per_step):
                if q_next is not None:
                    over_low(q_next, n // 2, n % 2, then)
            if last_bin + SIZE == 8 and q_last is not None:
                for tile in range(TILES):
                    back_low(q_last, tile, backs[ago % 2])
        return flight

    for tile in range(TILES):
        over_low(0, tile, 0, even)
        over_low(0, tile, 1, even)

    backs_of = ((even_back, odd_back), (odd_back, even_back))
    enter_of = ((even, odd), (odd, even))
    flight = held_entered[...], held_multiplied[...], held_turned[...]
    for q in range(2):
        phase_copy(q + 1).wait()
        flight = half(flight, enter_of[q][0], q + 1, enter_of[q][1], None, backs_of[q])
    held_entered[...], held_multiplied[...], held_turned[...] = flight

    def pair_step(t, carry):
        flight = held_entered[...], held_multiplied[...], held_turned[...]
        for n in range(2):
            phase_copy(2 * t + n + 1).wait()
        for n in range(2):
            q = 2 * t + n
            flight = half(flight, enter_of[n][0], q + 1, enter_of[n][1], q - delay, backs_of[n])
        held_entered[...], held_multiplied[...], held_turned[...] = flight
        return carry

    lax.fori_loop(1, 3, pair_step, 0, unroll=2)
    phase_copy(7).wait()
    flight = held_entered[...], held_multiplied[...], held_turned[...]
    for q in range(6, 8):
        after = q + 1 if q < 7 else None
        flight = half(flight, enter_of[q % 2][0], after, enter_of[q % 2][1], q - delay, backs_of[q % 2])
    for step in range(3):
        ago, last_bin = left_at(step)
        q = 8 - ago
        target = (even_back, odd_back)[q % 2]
        flight = advance(flight, None, 0, target, last_bin)
        if last_bin + SIZE == 8:
            for tile in range(TILES):
                back_low(q, tile, target)

    def gather_step(tile, carry):
        scale = 1.0 / LENGTH
        for b in range(8):
            column = []
            for q in range(8):
                at = 8 * b + q
                value = (gathered[tile, at, :, :LANES], gathered[tile, at, :, LANES:])
                column.append(turn(value, b * (q + 0.25) / 64.0))
            for a, (r, i) in enumerate(dft8(column, 1)):
                c, s = unit(a / 32.0)
                results[tile, slot_of(8 * a + b)] = r * (c * scale) - i * (s * scale)
        out_copy(tile).start()
        return carry

    lax.fori_loop(0, TILES, gather_step, 0)
    for i in range(TILES):
        out_copy(i).wait()


def side_by_side(turns):
    angle = 2.0 * np.pi * turns
    return np.concatenate([np.cos(angle), np.sin(angle)], axis=-1).astype(np.float32)


def outer_phases():
    position = np.arange(ROWS * LANES).reshape(1, ROWS, LANES)
    bins = np.arange(BLOCKS).reshape(8, 8).T.reshape(BLOCKS, 1, 1)
    turns = side_by_side(position * (bins + 0.25) / LENGTH)
    return turns.reshape(8, 8, ROWS, 2 * LANES)


def inner_phases():
    return side_by_side(np.outer(np.arange(ROWS), np.arange(LANES)) / (ROWS * LANES))


def halves(whole):
    high = whole.astype(np.float32).astype(ml_dtypes.bfloat16)
    low = (whole - high.astype(np.float64)).astype(np.float32).astype(ml_dtypes.bfloat16)
    return high, low


def rotation(size):
    angle = 2.0 * np.pi * (np.outer(np.arange(size), np.arange(size)) % size) / size
    c, s = np.cos(angle), np.sin(angle)
    return np.block([[c, s], [-s, c]])


def left_table():
    high, low = halves(rotation(ROWS))
    return np.block([[high, high], [low, np.zeros_like(low)]])


def right_table():
    high, low = halves(rotation(LANES).T)
    return np.concatenate([high, high, low], axis=0)


MIB = 1024 * 1024
PARAMS = pltpu.CompilerParams(vmem_limit_bytes=56 * MIB)


ANY = pl.BlockSpec(memory_space=pl.ANY)


def pack(signal, cotangent, long_filter, chips):
    groups = signal.shape[0] // TILE
    height = ROWS + ROWS // 2
    return pl.pallas_call(
        pack_kernel,
        in_specs=[ANY] * 3,
        out_specs=ANY,
        out_shape=jax.ShapeDtypeStruct((2, chips, height, LANES), jnp.float32),
        scratch_shapes=[
            pltpu.VMEM((groups, 3, TILE, ROWS * LANES), jnp.float32),
            pltpu.VMEM((groups, 2, TILE, height, LANES), jnp.float32),
            pltpu.SemaphoreType.DMA((groups, 3)),
            pltpu.SemaphoreType.DMA((chips // TILE, 3)),
        ],
        compiler_params=PARAMS,
        name="pack",
    )(signal, cotangent, long_filter)


def unpack(landed, channels):
    groups = channels // TILE
    result = jax.ShapeDtypeStruct((channels, ROWS * LANES), jnp.float32)
    return pl.pallas_call(
        unpack_kernel,
        in_specs=[ANY],
        out_specs=[ANY, ANY],
        out_shape=[result, result],
        scratch_shapes=[
            pltpu.VMEM((groups, 2, TILE, ROWS, LANES), jnp.float32),
            pltpu.VMEM((groups, 2, TILE, ROWS * LANES), jnp.float32),
            pltpu.SemaphoreType.DMA((groups, 2)),
            pltpu.SemaphoreType.DMA((groups, 2)),
        ],
        compiler_params=pltpu.CompilerParams(vmem_limit_bytes=16 * MIB),
        name="unpack",
    )(landed)


def correlate(core, arrived, swapped):
    tables = [
        outer_phases(),
        left_table(),
        inner_phases(),
        right_table(),
    ]
    tile = (TILES, BLOCKS, TILE, LANES)
    return pl.pallas_call(
        correlate_kernel,
        in_specs=[pl.BlockSpec(memory_space=pltpu.SMEM)] + [ANY] * (2 + len(tables)),
        out_specs=ANY,
        out_shape=jax.ShapeDtypeStruct((BLOCKS, ROWS, LANES), jnp.float32),
        scratch_shapes=[pltpu.VMEM(table.shape, table.dtype) for table in tables]
        + [
            pltpu.VMEM(tile, jnp.float32),
            pltpu.VMEM(tile, jnp.float32),
            pltpu.VMEM((2, TILES, BLOCKS, TILE, 2 * LANES), jnp.float32),
            pltpu.VMEM((8, 2, ROWS, 2 * LANES), jnp.float32),
            pltpu.VMEM((8, 2, ROWS, 2 * LANES), jnp.float32),
            pltpu.VMEM((8, ROWS, 2 * LANES), jnp.float32),
            pltpu.VMEM((8, ROWS, 2 * LANES), jnp.float32),
            pltpu.VMEM((TILES, BLOCKS, TILE, 2 * LANES), jnp.float32),
            pltpu.VMEM(tile, jnp.float32),
            pltpu.VMEM((2 * SIZE * ROWS, 2 * LANES), jnp.float32),
            pltpu.VMEM((SIZE * ROWS, 2 * LANES), jnp.float32),
            pltpu.VMEM((2 * ROWS, SIZE * LANES), jnp.float32),
            pltpu.SemaphoreType.DMA((TILES,)),
            pltpu.SemaphoreType.DMA((TILES,)),
            pltpu.SemaphoreType.DMA((len(tables),)),
            pltpu.SemaphoreType.DMA((8,)),
            pltpu.SemaphoreType.DMA((TILES,)),
        ],
        compiler_params=PARAMS,
        name="correlate",
    )(core, arrived, swapped, *tables)


def exchange(blocks):
    return lax.all_to_all(blocks, LISTED, split_axis=0, concat_axis=0, tiled=True)


def on_device(signal, cotangent, long_filter):
    channels = signal.shape[0]
    packed = pack(signal, cotangent, long_filter, BLOCKS // 2)
    arrived = exchange(packed.reshape(BLOCKS, *packed.shape[2:]))
    swapped = lax.ppermute(arrived[:, ROWS:], "core", [(0, 1), (1, 0)])
    core = lax.axis_index("core").astype(jnp.int32).reshape(1)
    landed = exchange(correlate(core, arrived, swapped))
    return tuple(unpack(landed.reshape(2, BLOCKS // 2, ROWS, LANES), channels))


def solution(mesh):
    digits = Mesh(mesh.devices.reshape(4, 4, 2, 2, 2), SEQUENCE + ("chan",))
    spec = P("chan", SEQUENCE)
    return jax.shard_map(
        on_device, mesh=digits, in_specs=(spec,) * 3, out_specs=(spec,) * 2, check_vma=False
    )
```

```python
import math

import jax
import jax.numpy as jnp
import ml_dtypes
import numpy as np
from jax import lax
from jax.experimental import pallas as pl
from jax.experimental.pallas import tpu as pltpu
from jax.sharding import Mesh, PartitionSpec as P

LANES = 128
BLOCKS = 64
ROWS = 64
TILE = 8
TILES = ROWS // TILE
HALF_TILES = TILES // 2
SIZE = 4
STEPS = 8 // SIZE
LENGTH = BLOCKS * ROWS * LANES
SEQUENCE = ("z", "y", "xh", "core")
LISTED = ("core", "z", "xh", "y")
ROOT_HALF = math.sqrt(0.5)


def slot_of(block):
    z, y, xh, core = block // 16, block // 4 % 4, block // 2 % 2, block % 2
    return 32 * core + 8 * z + 4 * xh + y


def unit(turns):
    return (math.cos(2.0 * math.pi * turns), math.sin(2.0 * math.pi * turns))


def plus(a, b):
    return (a[0] + b[0], a[1] + b[1])


def minus(a, b):
    return (a[0] - b[0], a[1] - b[1])


def turn(a, turns):
    turns = turns % 1.0
    if turns == 0.0:
        return a
    c, s = unit(turns)
    return (a[0] * c - a[1] * s, a[1] * c + a[0] * s)


def quarter(a, sign):
    if sign > 0:
        return (-a[1], a[0])
    return (a[1], -a[0])


def dft4(v, sign):
    t0, t1 = plus(v[0], v[2]), minus(v[0], v[2])
    t2, t3 = plus(v[1], v[3]), quarter(minus(v[1], v[3]), sign)
    return [plus(t0, t2), plus(t1, t3), minus(t0, t2), minus(t1, t3)]


def dft8(v, sign):
    up = [plus(v[n], v[n + 4]) for n in range(4)]
    down = [minus(v[n], v[n + 4]) for n in range(4)]
    r, i = down[1]
    down[1] = ((r - sign * i) * ROOT_HALF, (i + sign * r) * ROOT_HALF)
    down[2] = quarter(down[2], sign)
    r, i = down[3]
    down[3] = ((-r - sign * i) * ROOT_HALF, (sign * r - i) * ROOT_HALF)
    even, odd = dft4(up, sign), dft4(down, sign)
    return [even[k // 2] if k % 2 == 0 else odd[k // 2] for k in range(8)]


def split(rows):
    high = rows.astype(jnp.bfloat16)
    return high, (rows - high.astype(jnp.float32)).astype(jnp.bfloat16)


def times_right(rows, table):
    high, low = split(rows)
    return jnp.dot(
        jnp.concatenate([high, low, high], axis=1), table, preferred_element_type=jnp.float32
    )


def times_left(table, columns):
    high, low = split(columns)
    both = jnp.dot(
        table, jnp.concatenate([high, low], axis=0), preferred_element_type=jnp.float32
    )
    return both[: 2 * ROWS] + both[2 * ROWS :]


def pack_kernel(signal, cotangent, long_filter, out, taken, packed, in_sems, out_sems):
    groups = signal.shape[0] // TILE
    sources = (long_filter, signal, cotangent)

    def arrival(g, n):
        rows = pl.ds(TILE * g, TILE)
        return pltpu.make_async_copy(sources[n].at[rows], taken.at[g, n], in_sems.at[g, n])

    def departure(g, n):
        chips = pl.ds(TILE * g, TILE)
        if n < 2:
            rows = pl.ds(0, ROWS)
            source, target = packed.at[g, n, :, rows], out.at[n, chips, rows]
        else:
            rows = pl.ds(ROWS, ROWS // 2)
            source, target = packed.at[g, :, :, rows], out.at[:, chips, rows]
        return pltpu.make_async_copy(source, target, out_sems.at[g, n])

    for g in range(groups):
        for n in range(3):
            arrival(g, n).start()
    for g in range(groups):
        for n in range(3):
            arrival(g, n).wait()
            for u in range(TILES):
                slabs = [
                    taken[g, n, :, (TILE * u + v) * LANES : (TILE * u + v + 1) * LANES]
                    for v in range(TILE)
                ]
                turned = jnp.swapaxes(jnp.stack(slabs), 0, 1)
                if n < 2:
                    packed[g, n, :, TILE * u : TILE * (u + 1)] = turned
                else:
                    low = ROWS + TILE * (u % HALF_TILES)
                    packed[g, u // HALF_TILES, :, low : low + TILE] = turned
            departure(g, n).start()
    for g in range(groups):
        for n in range(3):
            departure(g, n).wait()


def unpack_kernel(landed, grad_signal, grad_filter, taken, turned_out, in_sems, out_sems):
    groups = grad_signal.shape[0] // TILE
    targets = (grad_signal, grad_filter)

    def arrival(g, n):
        chips = pl.ds(TILE * g, TILE)
        return pltpu.make_async_copy(landed.at[n, chips], taken.at[g, n], in_sems.at[g, n])

    def departure(g, n):
        rows = pl.ds(TILE * g, TILE)
        return pltpu.make_async_copy(turned_out.at[g, n], targets[n].at[rows], out_sems.at[g, n])

    for g in range(groups):
        for n in range(2):
            arrival(g, n).start()
    for g in range(groups):
        for n in range(2):
            arrival(g, n).wait()
            for u in range(TILES):
                turned = jnp.swapaxes(taken[g, n, :, TILE * u : TILE * (u + 1)], 0, 1)
                for v in range(TILE):
                    at = (TILE * u + v) * LANES
                    turned_out[g, n, :, at : at + LANES] = turned[v]
            departure(g, n).start()
    for g in range(groups):
        for n in range(2):
            departure(g, n).wait()


def correlate_kernel(core, arrived, swapped, *refs):
    tables, out, copies = refs[:4], refs[4], refs[5:9]
    phases, left, inner, right = copies
    own, other, spread, even, odd, even_back, odd_back, gathered, results = refs[9:18]
    held_entered, held_multiplied, held_turned = refs[18:21]
    own_sems, other_sems, table_sems, phase_sems, out_sems = refs[21:]
    offset = HALF_TILES * core[0]

    def tile_rows(tile):
        if isinstance(tile, int):
            return slice(tile * TILE, (tile + 1) * TILE)
        return pl.ds(pl.multiple_of(tile * TILE, TILE), TILE)

    def own_copy(i):
        return pltpu.make_async_copy(arrived.at[:, pl.ds(TILE * i, TILE)], own.at[i], own_sems.at[i])

    def other_copy(i):
        if i < HALF_TILES:
            source = arrived.at[:, pl.ds(ROWS + TILE * i, TILE)]
        else:
            source = swapped.at[:, pl.ds(TILE * (i - HALF_TILES), TILE)]
        return pltpu.make_async_copy(source, other.at[(i + offset) % TILES], other_sems.at[i])

    def table_copy(n):
        return pltpu.make_async_copy(tables[n], copies[n], table_sems.at[n])

    def phase_copy(q):
        return pltpu.make_async_copy(tables[0].at[q], phases.at[q], phase_sems.at[q])

    def out_copy(i):
        return pltpu.make_async_copy(results.at[i], out.at[:, tile_rows(i)], out_sems.at[i])

    for i in range(TILES):
        own_copy(i).start()
        other_copy(i).start()
    for n in range(1, len(tables)):
        table_copy(n).start()
    for q in range(3):
        phase_copy(q).start()
    for ref in (held_entered, held_multiplied, held_turned, even_back, odd_back):
        ref[...] = jnp.zeros(ref.shape, ref.dtype)

    def over_high(source, slot, number):
        for b in range(8):
            column = []
            for a in range(8):
                c, s = unit(-a / 32.0)
                x = source[slot, slot_of(8 * a + b)]
                column.append((x * c, x * s))
            for q, value in enumerate(dft8(column, -1)):
                r, i = turn(value, -b * (q + 0.25) / 64.0)
                spread[number, slot, 8 * b + q, :, :LANES] = r
                spread[number, slot, 8 * b + q, :, LANES:] = i

    def spread_step(i, carry):
        slot = (i + offset) % TILES
        pltpu.make_async_copy(arrived.at[:, pl.ds(0, TILE)], own.at[i], own_sems.at[i]).wait()
        over_high(own, i, 0)
        pltpu.make_async_copy(arrived.at[:, pl.ds(0, TILE)], other.at[slot], other_sems.at[i]).wait()
        over_high(other, slot, 1)
        return carry

    lax.fori_loop(0, TILES, spread_step, 0)
    for n in range(1, len(tables)):
        table_copy(n).wait()
    for q in range(3, 8):
        phase_copy(q).start()
    phase_copy(0).wait()

    def over_low(q, tile, number, target):
        rows = tile_rows(tile)
        column = []
        for b in range(8):
            at = 8 * b + q
            column.append((spread[number, tile, at, :, :LANES], spread[number, tile, at, :, LANES:]))
        for p, (r, i) in enumerate(dft8(column, -1)):
            c, s = phases[q, p, rows, :LANES], phases[q, p, rows, LANES:]
            target[p, number, rows, :LANES] = r * c + i * s
            target[p, number, rows, LANES:] = i * c - r * s

    def back_low(q, tile, source):
        rows = tile_rows(tile)
        column = []
        for p in range(8):
            r, i = source[p, rows, :LANES], source[p, rows, LANES:]
            c, s = phases[q, p, rows, :LANES], phases[q, p, rows, LANES:]
            column.append((r * c - i * s, i * c + r * s))
        for b, (r, i) in enumerate(dft8(column, 1)):
            gathered[tile, 8 * b + q, :, :LANES] = r
            gathered[tile, 8 * b + q, :, LANES:] = i

    c_inner, s_inner = inner[:, :LANES], inner[:, LANES:]

    def entry_columns(source, first_bin):
        columns = []
        for e in range(SIZE):
            for number in range(2):
                x = source[first_bin + e, number]
                columns.append(jnp.concatenate([x[:, :LANES], x[:, LANES:]], axis=0))
        return columns

    def lanes(y, n):
        at = slice(n * LANES, (n + 1) * LANES)
        return y[:ROWS, at], y[ROWS:, at]

    def entry_rows(y):
        rows = []
        for n in range(2 * SIZE):
            r, i = lanes(y, n)
            rows.append(
                jnp.concatenate(
                    [r * c_inner + i * s_inner, i * c_inner - r * s_inner], axis=1
                )
            )
        return jnp.concatenate(rows, axis=0)

    def product_rows(z):
        made = []
        for e in range(SIZE):
            f = z[2 * e * ROWS : (2 * e + 1) * ROWS]
            g = z[(2 * e + 1) * ROWS : (2 * e + 2) * ROWS]
            fr, fi, gr, gi = f[:, :LANES], f[:, LANES:], g[:, :LANES], g[:, LANES:]
            made.append(jnp.concatenate([gi * fr - gr * fi, gr * fr + gi * fi], axis=1))
        return jnp.concatenate(made, axis=0)

    def exit_columns(z):
        columns = []
        for e in range(SIZE):
            i = z[e * ROWS : (e + 1) * ROWS, :LANES]
            r = z[e * ROWS : (e + 1) * ROWS, LANES:]
            columns.append(
                jnp.concatenate(
                    [i * c_inner + r * s_inner, r * c_inner - i * s_inner], axis=0
                )
            )
        return jnp.concatenate(columns, axis=1)

    def leave(target, first_bin, y, start):
        for e in range(SIZE):
            i, r = lanes(y, start + e)
            target[first_bin + e, :, :LANES] = r
            target[first_bin + e, :, LANES:] = i

    def advance(flight, source, first_bin, target, last_bin):
        entered, multiplied, turned = flight
        leave(target, last_bin, times_left(left[...], turned), 0)
        turned = exit_columns(times_right(multiplied, right[...]))
        multiplied = product_rows(times_right(entered, right[...]))
        if source is not None:
            columns = jnp.concatenate(entry_columns(source, first_bin), axis=1)
            entered = entry_rows(times_left(left[...], columns))
        return entered, multiplied, turned

    def left_at(step):
        return -((step - 3) // STEPS), (step - 3) % STEPS * SIZE

    delay = next(ago for ago, at in map(left_at, range(STEPS)) if at + SIZE == 8)

    def half(flight, now, q_next, then, q_last, backs):
        per_step = 2 * TILES // STEPS
        for step in range(STEPS):
            ago, last_bin = left_at(step)
            flight = advance(flight, now, step * SIZE, backs[ago % 2], last_bin)
            for n in range(step * per_step, (step + 1) * per_step):
                if q_next is not None:
                    over_low(q_next, n // 2, n % 2, then)
            if last_bin + SIZE == 8 and q_last is not None:
                for tile in range(TILES):
                    back_low(q_last, tile, backs[ago % 2])
        return flight

    for tile in range(TILES):
        over_low(0, tile, 0, even)
        over_low(0, tile, 1, even)

    backs_of = ((even_back, odd_back), (odd_back, even_back))
    enter_of = ((even, odd), (odd, even))
    flight = held_entered[...], held_multiplied[...], held_turned[...]
    for q in range(2):
        phase_copy(q + 1).wait()
        flight = half(flight, enter_of[q][0], q + 1, enter_of[q][1], None, backs_of[q])
    held_entered[...], held_multiplied[...], held_turned[...] = flight

    def pair_step(t, carry):
        flight = held_entered[...], held_multiplied[...], held_turned[...]
        for n in range(2):
            phase_copy(2 * t + n + 1).wait()
        for n in range(2):
            q = 2 * t + n
            flight = half(flight, enter_of[n][0], q + 1, enter_of[n][1], q - delay, backs_of[n])
        held_entered[...], held_multiplied[...], held_turned[...] = flight
        return carry

    lax.fori_loop(1, 3, pair_step, 0, unroll=2)
    phase_copy(7).wait()
    flight = held_entered[...], held_multiplied[...], held_turned[...]
    for q in range(6, 8):
        after = q + 1 if q < 7 else None
        flight = half(flight, enter_of[q % 2][0], after, enter_of[q % 2][1], q - delay, backs_of[q % 2])
    for step in range(3):
        ago, last_bin = left_at(step)
        q = 8 - ago
        target = (even_back, odd_back)[q % 2]
        flight = advance(flight, None, 0, target, last_bin)
        if last_bin + SIZE == 8:
            for tile in range(TILES):
                back_low(q, tile, target)

    def gather_step(tile, carry):
        scale = 1.0 / LENGTH
        for b in range(8):
            column = []
            for q in range(8):
                at = 8 * b + q
                value = (gathered[tile, at, :, :LANES], gathered[tile, at, :, LANES:])
                column.append(turn(value, b * (q + 0.25) / 64.0))
            for a, (r, i) in enumerate(dft8(column, 1)):
                c, s = unit(a / 32.0)
                results[tile, slot_of(8 * a + b)] = r * (c * scale) - i * (s * scale)
        out_copy(tile).start()
        return carry

    lax.fori_loop(0, TILES, gather_step, 0)
    for i in range(TILES):
        out_copy(i).wait()


def side_by_side(turns):
    angle = 2.0 * np.pi * turns
    return np.concatenate([np.cos(angle), np.sin(angle)], axis=-1).astype(np.float32)


def outer_phases():
    position = np.arange(ROWS * LANES).reshape(1, ROWS, LANES)
    bins = np.arange(BLOCKS).reshape(8, 8).T.reshape(BLOCKS, 1, 1)
    turns = side_by_side(position * (bins + 0.25) / LENGTH)
    return turns.reshape(8, 8, ROWS, 2 * LANES)


def inner_phases():
    return side_by_side(np.outer(np.arange(ROWS), np.arange(LANES)) / (ROWS * LANES))


def halves(whole):
    high = whole.astype(np.float32).astype(ml_dtypes.bfloat16)
    low = (whole - high.astype(np.float64)).astype(np.float32).astype(ml_dtypes.bfloat16)
    return high, low


def rotation(size):
    angle = 2.0 * np.pi * (np.outer(np.arange(size), np.arange(size)) % size) / size
    c, s = np.cos(angle), np.sin(angle)
    return np.block([[c, s], [-s, c]])


def left_table():
    high, low = halves(rotation(ROWS))
    return np.block([[high, high], [low, np.zeros_like(low)]])


def right_table():
    high, low = halves(rotation(LANES).T)
    return np.concatenate([high, high, low], axis=0)


MIB = 1024 * 1024
PARAMS = pltpu.CompilerParams(vmem_limit_bytes=56 * MIB)


ANY = pl.BlockSpec(memory_space=pl.ANY)


def pack(signal, cotangent, long_filter, chips):
    groups = signal.shape[0] // TILE
    height = ROWS + ROWS // 2
    return pl.pallas_call(
        pack_kernel,
        in_specs=[ANY] * 3,
        out_specs=ANY,
        out_shape=jax.ShapeDtypeStruct((2, chips, height, LANES), jnp.float32),
        scratch_shapes=[
            pltpu.VMEM((groups, 3, TILE, ROWS * LANES), jnp.float32),
            pltpu.VMEM((groups, 2, TILE, height, LANES), jnp.float32),
            pltpu.SemaphoreType.DMA((groups, 3)),
            pltpu.SemaphoreType.DMA((groups, 3)),
        ],
        compiler_params=PARAMS,
        name="pack",
    )(signal, cotangent, long_filter)


def unpack(landed, channels):
    groups = channels // TILE
    result = jax.ShapeDtypeStruct((channels, ROWS * LANES), jnp.float32)
    return pl.pallas_call(
        unpack_kernel,
        in_specs=[ANY],
        out_specs=[ANY, ANY],
        out_shape=[result, result],
        scratch_shapes=[
            pltpu.VMEM((groups, 2, TILE, ROWS, LANES), jnp.float32),
            pltpu.VMEM((groups, 2, TILE, ROWS * LANES), jnp.float32),
            pltpu.SemaphoreType.DMA((groups, 2)),
            pltpu.SemaphoreType.DMA((groups, 2)),
        ],
        compiler_params=pltpu.CompilerParams(vmem_limit_bytes=16 * MIB),
        name="unpack",
    )(landed)


def correlate(core, arrived, swapped):
    tables = [
        outer_phases(),
        left_table(),
        inner_phases(),
        right_table(),
    ]
    tile = (TILES, BLOCKS, TILE, LANES)
    return pl.pallas_call(
        correlate_kernel,
        in_specs=[pl.BlockSpec(memory_space=pltpu.SMEM)] + [ANY] * (2 + len(tables)),
        out_specs=ANY,
        out_shape=jax.ShapeDtypeStruct((BLOCKS, ROWS, LANES), jnp.float32),
        scratch_shapes=[pltpu.VMEM(table.shape, table.dtype) for table in tables]
        + [
            pltpu.VMEM(tile, jnp.float32),
            pltpu.VMEM(tile, jnp.float32),
            pltpu.VMEM((2, TILES, BLOCKS, TILE, 2 * LANES), jnp.float32),
            pltpu.VMEM((8, 2, ROWS, 2 * LANES), jnp.float32),
            pltpu.VMEM((8, 2, ROWS, 2 * LANES), jnp.float32),
            pltpu.VMEM((8, ROWS, 2 * LANES), jnp.float32),
            pltpu.VMEM((8, ROWS, 2 * LANES), jnp.float32),
            pltpu.VMEM((TILES, BLOCKS, TILE, 2 * LANES), jnp.float32),
            pltpu.VMEM(tile, jnp.float32),
            pltpu.VMEM((2 * SIZE * ROWS, 2 * LANES), jnp.float32),
            pltpu.VMEM((SIZE * ROWS, 2 * LANES), jnp.float32),
            pltpu.VMEM((2 * ROWS, SIZE * LANES), jnp.float32),
            pltpu.SemaphoreType.DMA((TILES,)),
            pltpu.SemaphoreType.DMA((TILES,)),
            pltpu.SemaphoreType.DMA((len(tables),)),
            pltpu.SemaphoreType.DMA((8,)),
            pltpu.SemaphoreType.DMA((TILES,)),
        ],
        compiler_params=PARAMS,
        name="correlate",
    )(core, arrived, swapped, *tables)


def exchange(blocks):
    return lax.all_to_all(blocks, LISTED, split_axis=0, concat_axis=0, tiled=True)


def on_device(signal, cotangent, long_filter):
    channels = signal.shape[0]
    packed = pack(signal, cotangent, long_filter, BLOCKS // 2)
    arrived = exchange(packed.reshape(BLOCKS, *packed.shape[2:]))
    swapped = lax.ppermute(arrived[:, ROWS:], "core", [(0, 1), (1, 0)])
    core = lax.axis_index("core").astype(jnp.int32).reshape(1)
    landed = exchange(correlate(core, arrived, swapped))
    return tuple(unpack(landed.reshape(2, BLOCKS // 2, ROWS, LANES), channels))


def solution(mesh):
    digits = Mesh(mesh.devices.reshape(4, 4, 2, 2, 2), SEQUENCE + ("chan",))
    spec = P("chan", SEQUENCE)
    return jax.shard_map(
        on_device, mesh=digits, in_specs=(spec,) * 3, out_specs=(spec,) * 2, check_vma=False
    )
```
